32 devices in a mesh: parts: 2 (over y), gy: 8 (over z, x), gx: 2 (over core).
Axes of the slice: x: 2, y: 2, z: 4, core: 2. Of those that a mesh axis runs over, the one named last changes fastest.
Arguments:
- activations: bfloat16 [64, 16384], P(('parts', 'gy'), 'gx'), parts along dimension 0, may hold values from -6 to 6
- qkv_weight: bfloat16 [4, 2304, 16384], P(None, 'gy', 'gx'), may hold values from -0.046875 to 0.046875
- out_weight: bfloat16 [16384, 8192], P('gy', 'gx'), may hold values from -0.0625 to 0.0625
- key_cache: bfloat16 [64, 4, 512, 128], P(('parts', 'gy'), 'gx'), parts along dimension 0, may hold values from -360 to 360
- value_cache: bfloat16 [64, 4, 512, 128], P(('parts', 'gy'), 'gx'), parts along dimension 0, may hold values from -6 to 6
- lengths: int32 [64], P(('parts', 'gy')), parts along dimension 0, may hold values from 1 to 512, as said below
Outputs:
- attn_out: bfloat16 [64, 16384], P(('parts', 'gx'), 'gy'), parts along dimension 0
The draws below stay inside these ranges and needn't reach their ends.
There are 2 independent parts, one for each index of `parts`. The reference program is written for one: setup_inputs(seed, part) draws one part's arguments, and reference() takes and returns one part's arrays. A program takes and returns all parts, laid end to end along the dimension named above; an argument that names none is the same for every part. Nothing has to cross between parts.
Inputs may be any that keep to these rules, and one draw needn't show every extreme that they name: Sequence b uses cache slots 0 to lengths[b] - 1; at least one sequence has exactly 512.
All inputs are finite; a program needn't handle non-finite values.
Results may differ from the reference program's by a relative error of at most 0.012.
The reference program's roundings to bfloat16 on the way count: a program that leaves them out, or rounds other values in their place, can miss the bound.
Values may be sent and summed in bfloat16 or wider, within the bound.
No kernel may reach another device: no remote copies, remote signals or barrier semaphores. Data moves between devices by JAX's collectives and lax.ppermute only.
A program may use at most 128 MiB of HBM per device.

```python
import jax
import jax.numpy as jnp
from jax import lax

D = 16384
HD = 128
KVH = 4
GROUP = 16
CACHE = 512
COLS = 2304
FEATS = 8192
SEQS = 32
N_GX = 2


def draw_key_cache(key, part):
    key = jax.random.fold_in(key, 11)
    first_key = jax.random.fold_in(key, 0)
    base = jnp.clip(jax.random.normal(first_key, (SEQS, KVH, CACHE, HD), jnp.float32), -6.0, 6.0)
    return base.astype(jnp.bfloat16)


def draw_lengths(key, part):
    key = jax.random.fold_in(key, 5)
    first_key, second_key = jax.random.split(key)
    raw_draw = jax.random.randint(first_key, (SEQS,), 0, CACHE, jnp.int32)
    spans = 1 + raw_draw * raw_draw // CACHE
    longest = jax.random.randint(second_key, (), 0, SEQS, jnp.int32)
    return spans.at[longest].set(CACHE)


def shard_levels(key, shape, shards, least, top_value):
    gain, own = 1.0, jax.random.fold_in(key, 6)
    for axis_at, shards_of in shards:
        draws = jnp.exp(jax.random.uniform(jax.random.fold_in(own, axis_at), (shards_of,), jnp.float32, least / len(shards), top_value / len(shards)))
        gain = gain * jnp.repeat(draws, shape[axis_at] // shards_of).reshape([-1 if axis == axis_at else 1 for axis in range(len(shape))])
    return gain


def scatter_about(rng, extent, scale, limit, pieces=(), kind=jnp.bfloat16):
    result = jax.random.normal(rng, extent, jnp.float32) * scale
    if len(pieces) > 0:
        result = shard_levels(rng, extent, pieces, -0.22, 0.18) * result
    return jnp.clip(result, min=-limit, max=limit).astype(kind)


def setup_inputs(seed: int = 0, part: int = 0) -> dict:
    arg_keys = jax.random.split(jax.random.key(seed), 7)
    part_keys = jax.random.split(jax.random.fold_in(arg_keys[6], part), 7)
    return {
        "activations": scatter_about(part_keys[0], (SEQS, D), 1.0, 6.0, ((0, 8), (1, 2))),
        "qkv_weight": scatter_about(arg_keys[1], (KVH, COLS, D), D ** -0.5, 0.046875, ((1, 8), (2, 2))),
        "out_weight": scatter_about(arg_keys[2], (D, FEATS), FEATS ** -0.5, 0.0625, ((0, 8), (1, 2))),
        "key_cache": draw_key_cache(jax.random.fold_in(jax.random.fold_in(arg_keys[6], part), 71), part),
        "value_cache": scatter_about(part_keys[4], (SEQS, KVH, CACHE, HD), 1.0, 6.0, ((0, 8), (1, 2))),
        "lengths": draw_lengths(jax.random.fold_in(jax.random.fold_in(arg_keys[6], part), 71), part),
    }


NEG_FILL = -1e30


def split_product(left, right):
    total = jnp.zeros((left.shape[0], right.shape[0]), jnp.float32)
    half_width = left.shape[1] // N_GX
    for half_index in range(N_GX):
        lower = half_index * half_width
        piece_sum = jnp.dot(left[:, lower:lower + half_width], right[:, lower:lower + half_width].T, preferred_element_type=jnp.float32).astype(jnp.bfloat16)
        total = total + lax.optimization_barrier(piece_sum).astype(jnp.float32)
    return total.astype(jnp.bfloat16)


def attend(joined, key_cache, value_cache, lengths):
    seq_count = joined.shape[0]
    queries = joined[:, :, :GROUP * HD].reshape(seq_count, KVH, GROUP, HD).astype(jnp.float32)
    new_key = joined[:, :, GROUP * HD:(GROUP + 1) * HD].astype(jnp.float32)
    new_value = joined[:, :, (GROUP + 1) * HD:].astype(jnp.float32)
    score_scale = HD ** -0.5
    scores = jnp.einsum('bkgh,bkth->bkgt', queries, key_cache.astype(jnp.float32)) * score_scale
    own = jnp.einsum('bkgh,bkh->bkg', queries, new_key) * score_scale
    positions = jnp.arange(key_cache.shape[2], dtype=jnp.int32)
    live = positions[None, None, None, :] < lengths.astype(jnp.int32)[:, None, None, None]
    scores = jnp.where(live, scores, NEG_FILL)
    top = jnp.maximum(jnp.max(scores, axis=3), own)
    weights = jnp.where(live, jnp.exp(scores - top[..., None]), 0.0)
    own_weight = jnp.exp(own - top)
    denom = jnp.sum(weights, axis=3) + own_weight
    weights = (weights / denom[..., None]).astype(jnp.bfloat16)
    own_weight = (own_weight / denom).astype(jnp.bfloat16)
    mixed = jnp.einsum('bkgt,bkth->bkgh', weights.astype(jnp.float32), value_cache.astype(jnp.float32))
    mixed = mixed + own_weight.astype(jnp.float32)[..., None] * new_value[:, :, None, :]
    return mixed.astype(jnp.bfloat16).reshape(seq_count, KVH * GROUP * HD)


def reference(activations, qkv_weight, out_weight, key_cache, value_cache, lengths):
    seq_count = activations.shape[0]
    flat_weight = qkv_weight.reshape(KVH * COLS, D)
    joined = split_product(activations, flat_weight).reshape(seq_count, KVH, COLS)
    attended = attend(joined, key_cache, value_cache, lengths)
    return split_product(attended, out_weight)
```

```python
import functools

import jax
import jax.numpy as jnp
from jax import lax
from jax.experimental import pallas as pl
from jax.experimental.pallas import tpu as pltpu
from jax.sharding import PartitionSpec as P

HD = 128
GROUP = 16
MIB = 1 << 20
NEG_FILL = -1e30
NT = (((1,), (1,)), ((), ()))


def normalize(scores, own_score, live):
    scores = jnp.where(live, scores, NEG_FILL)
    top = jnp.maximum(jnp.max(scores, axis=3), own_score)
    weights = jnp.where(live, jnp.exp(scores - top[..., None]), 0.0)
    own_weight = jnp.exp(own_score - top)
    denom = jnp.sum(weights, axis=3) + own_weight
    return (
        (weights / denom[..., None]).astype(jnp.bfloat16),
        (own_weight / denom).astype(jnp.bfloat16),
    )


def local_plain(activations, qkv_weight, out_weight, key_cache, value_cache, lengths):
    head_count, col_part, half_width = qkv_weight.shape
    flat_weight = qkv_weight.reshape(head_count * col_part, half_width)
    row_piece = lax.all_gather(activations, "gy", axis=0, tiled=True)
    product = lax.dot_general(row_piece, flat_weight, NT, preferred_element_type=jnp.float32)
    partial_value = product.reshape(row_piece.shape[0], head_count, col_part)
    summed = lax.psum_scatter(
        partial_value.astype(jnp.bfloat16), "gx", scatter_dimension=1, tiled=True
    )
    joined = lax.all_to_all(summed, "gy", split_axis=0, concat_axis=2, tiled=True)
    seq_local, kv_local, cache_len = (key_cache.shape[0], key_cache.shape[1], key_cache.shape[2])
    queries = joined[:, :, : GROUP * HD].reshape(seq_local, kv_local, GROUP, HD)
    new_key = joined[:, :, GROUP * HD : (GROUP + 1) * HD]
    new_value = joined[:, :, (GROUP + 1) * HD :]
    score_scale = HD ** (-0.5)
    own_score = (
        jnp.einsum("skgh,skh->skg", queries, new_key, preferred_element_type=jnp.float32)
        * score_scale
    )
    positions = jnp.arange(cache_len, dtype=jnp.int32)
    live = positions[None, None, None, :] < lengths[:, None, None, None]
    scores = (
        jnp.einsum("skgh,skth->skgt", queries, key_cache, preferred_element_type=jnp.float32)
        * score_scale
    )
    weights, own_weight = normalize(scores, own_score, live)
    mixed = jnp.einsum("skgt,skth->skgh", weights, value_cache, preferred_element_type=jnp.float32)
    mixed = (
        mixed
        + own_weight.astype(jnp.float32)[..., None] * new_value.astype(jnp.float32)[:, :, None, :]
    )
    attended = mixed.astype(jnp.bfloat16).reshape(seq_local, kv_local * GROUP * HD)
    terms = lax.dot_general(
        lax.all_gather(attended, "gy", axis=0, tiled=True),
        out_weight,
        NT,
        preferred_element_type=jnp.float32,
    )
    return lax.psum_scatter(terms.astype(jnp.bfloat16), "gx", scatter_dimension=0, tiled=True)


def swap(x):
    return lax.ppermute(x, "gx", [(0, 1), (1, 0)])


def hop(x, chips, step):
    half = chips // 2
    pairs = []
    for chip in range(chips):
        for core in range(2):
            pairs.append((2 * chip + core, 2 * (chip ^ (step + core * half)) + core))
    return lax.ppermute(x, ("gy", "gx"), pairs)


def gather_rows(block, chips):
    rows = block.shape[0]
    both = jnp.concatenate([block, swap(block)], axis=0)
    got = [hop(both, chips, step) for step in range(chips // 2)]
    theirs = swap(jnp.concatenate([piece[rows:] for piece in got], axis=0))
    return jnp.concatenate([piece[:rows] for piece in got] + [theirs], axis=0)


def project_kernel(x_ref, w_ref, keep_ref, send_ref):
    half = keep_ref.shape[1]
    for head in range(w_ref.shape[0]):
        value = lax.dot_general(x_ref[...], w_ref[head], NT, preferred_element_type=jnp.float32)
        value = value.astype(jnp.bfloat16)
        keep_ref[head] = value[:half]
        send_ref[head] = value[half:]


def attend_kernel(place_ref, lengths_ref, mine_ref, theirs_ref, key_ref, value_ref, out_ref, wide, tall):
    chips = 2 * mine_ref.shape[0]
    seqs, heads, slots = key_ref.shape[0], key_ref.shape[1], key_ref.shape[2]
    part = mine_ref.shape[3]
    chip, core = place_ref[0], place_ref[1]
    half = chips // 2
    for head in range(heads):
        at = core * heads + head
        for other in range(chips):
            mask = chip ^ other
            step = mask & (half - 1)
            near = (mask // half) == core
            piece = jnp.where(
                near,
                mine_ref[step, at].astype(jnp.float32),
                theirs_ref[step, at].astype(jnp.float32),
            )
            wide[:, other * part : (other + 1) * part] = piece
        for column in range(GROUP + 2):
            tall[head, :, column, :] = wide[:, column * HD : (column + 1) * HD]
    scale = HD ** (-0.5)
    position = lax.broadcasted_iota(jnp.int32, (GROUP, slots), 1)
    for seq in range(seqs):
        live = position < lengths_ref[seq]
        for head in range(heads):
            query = tall[head, seq, :GROUP, :]
            new_key = tall[head, seq, GROUP : GROUP + 1, :]
            new_value = tall[head, seq, GROUP + 1 : GROUP + 2, :]
            own = jnp.sum(query * new_key, axis=1, keepdims=True) * scale
            scores = lax.dot_general(
                query.astype(jnp.bfloat16), key_ref[seq, head], NT, preferred_element_type=jnp.float32
            )
            scores = jnp.where(live, scores * scale, NEG_FILL)
            top = jnp.maximum(jnp.max(scores, axis=1, keepdims=True), own)
            weights = jnp.where(live, jnp.exp(scores - top), 0.0)
            own_weight = jnp.exp(own - top)
            denom = jnp.sum(weights, axis=1, keepdims=True) + own_weight
            weights = (weights / denom).astype(jnp.bfloat16)
            own_weight = (own_weight / denom).astype(jnp.bfloat16).astype(jnp.float32)
            mixed = jnp.dot(weights, value_ref[seq, head], preferred_element_type=jnp.float32)
            mixed = mixed + own_weight * new_value
            for query_head in range(GROUP):
                column = (head * GROUP + query_head) * HD
                wide2 = mixed[query_head : query_head + 1]
                out_ref[seq : seq + 1, column : column + HD] = wide2


def output_kernel(place_ref, x_ref, w_ref, keep_ref, send_ref, *, rows):
    total = x_ref.shape[0]
    half = total // 2
    row = lax.broadcasted_iota(jnp.int32, (total, total), 0)
    column = lax.broadcasted_iota(jnp.int32, (total, total), 1)
    order = jnp.where((row ^ (place_ref[0] * rows)) == column, 1.0, 0.0).astype(jnp.bfloat16)
    x = jnp.dot(order, x_ref[...], preferred_element_type=jnp.float32).astype(jnp.bfloat16)
    value = lax.dot_general(x, w_ref[...], NT, preferred_element_type=jnp.float32)
    value = value.astype(jnp.bfloat16)
    keep_ref[...] = value[:half]
    send_ref[...] = value[half:]


def in_vmem(count):
    return [pl.BlockSpec(memory_space=pltpu.VMEM)] * count


def in_smem(count):
    return [pl.BlockSpec(memory_space=pltpu.SMEM)] * count


def hold(x):
    return pltpu.with_memory_space_constraint(x, pltpu.VMEM)


def local(activations, qkv_weight, out_weight, key_cache, value_cache, lengths, *, chips):
    heads, part, _ = qkv_weight.shape
    seqs, kv_local, slots, _ = key_cache.shape
    out_cols = out_weight.shape[0]
    half = chips // 2 * seqs
    place = jnp.stack([lax.axis_index("gy"), lax.axis_index("gx")]).astype(jnp.int32)

    x = gather_rows(activations, chips)
    piece = jax.ShapeDtypeStruct((heads, half, part), jnp.bfloat16)
    keep, send = pl.pallas_call(
        project_kernel,
        out_shape=(piece, piece),
        in_specs=in_vmem(2),
        out_specs=tuple(in_vmem(2)),
        compiler_params=pltpu.CompilerParams(vmem_limit_bytes=8 * MIB),
        name="project",
    )(hold(x), hold(qkv_weight))
    joined = (keep.astype(jnp.float32) + swap(send).astype(jnp.float32)).astype(jnp.bfloat16)
    got = [hop(joined[:, step * seqs : (step + 1) * seqs], chips, step) for step in range(chips // 2)]
    mine = jnp.stack(got)
    theirs = swap(mine)

    feats = kv_local * GROUP * HD
    attended = pl.pallas_call(
        attend_kernel,
        out_shape=jax.ShapeDtypeStruct((seqs, feats), jnp.float32),
        in_specs=in_smem(2) + in_vmem(4),
        out_specs=in_vmem(1)[0],
        scratch_shapes=[
            pltpu.VMEM((seqs, chips * part), jnp.float32),
            pltpu.VMEM((kv_local, seqs, GROUP + 8, HD), jnp.float32),
        ],
        compiler_params=pltpu.CompilerParams(vmem_limit_bytes=8 * MIB),
        name="attend",
    )(place, lengths, hold(mine), hold(theirs), hold(key_cache), hold(value_cache))
    attended = attended.astype(jnp.bfloat16)

    x = gather_rows(attended, chips)
    piece = jax.ShapeDtypeStruct((half, out_cols), jnp.bfloat16)
    keep, send = pl.pallas_call(
        functools.partial(output_kernel, rows=seqs),
        out_shape=(piece, piece),
        in_specs=in_smem(1) + in_vmem(2),
        out_specs=tuple(in_vmem(2)),
        compiler_params=pltpu.CompilerParams(vmem_limit_bytes=8 * MIB),
        name="output",
    )(place, hold(x), hold(out_weight))
    return (keep.astype(jnp.float32) + swap(send).astype(jnp.float32)).astype(jnp.bfloat16)


def solution(mesh):
    in_specs = (
        P(("parts", "gy"), "gx"),
        P(None, "gy", "gx"),
        P("gy", "gx"),
        P(("parts", "gy"), "gx", None, None),
        P(("parts", "gy"), "gx", None, None),
        P(("parts", "gy")),
    )
    out_specs = P(("parts", "gx"), "gy")
    chips = mesh.shape["gy"]

    def whole(activations, qkv_weight, *rest):
        part = qkv_weight.shape[1] // chips
        seqs = activations.shape[0] // (mesh.shape["parts"] * chips)
        paired = mesh.shape["gx"] == 2 and chips in (2, 4, 8, 16) and part % 16 == 0
        paired = paired and seqs & (seqs - 1) == 0 and (chips // 2 * seqs) % 16 == 0
        body = functools.partial(local, chips=chips) if paired else local_plain
        return jax.shard_map(
            body, mesh=mesh, in_specs=in_specs, out_specs=out_specs, check_vma=False
        )(activations, qkv_weight, *rest)

    return whole
```

```python
import functools

import jax
import jax.numpy as jnp
from jax import lax
from jax.experimental import pallas as pl
from jax.experimental.pallas import tpu as pltpu
from jax.sharding import PartitionSpec as P

HD = 128
GROUP = 16
MIB = 1 << 20
NEG_FILL = -1e30
NT = (((1,), (1,)), ((), ()))


def normalize(scores, own_score, live):
    scores = jnp.where(live, scores, NEG_FILL)
    top = jnp.maximum(jnp.max(scores, axis=3), own_score)
    weights = jnp.where(live, jnp.exp(scores - top[..., None]), 0.0)
    own_weight = jnp.exp(own_score - top)
    denom = jnp.sum(weights, axis=3) + own_weight
    return (
        (weights / denom[..., None]).astype(jnp.bfloat16),
        (own_weight / denom).astype(jnp.bfloat16),
    )


def local_plain(activations, qkv_weight, out_weight, key_cache, value_cache, lengths):
    head_count, col_part, half_width = qkv_weight.shape
    flat_weight = qkv_weight.reshape(head_count * col_part, half_width)
    row_piece = lax.all_gather(activations, "gy", axis=0, tiled=True)
    product = lax.dot_general(row_piece, flat_weight, NT, preferred_element_type=jnp.float32)
    partial_value = product.reshape(row_piece.shape[0], head_count, col_part)
    summed = lax.psum_scatter(
        partial_value.astype(jnp.bfloat16), "gx", scatter_dimension=1, tiled=True
    )
    joined = lax.all_to_all(summed, "gy", split_axis=0, concat_axis=2, tiled=True)
    seq_local, kv_local, cache_len = (key_cache.shape[0], key_cache.shape[1], key_cache.shape[2])
    queries = joined[:, :, : GROUP * HD].reshape(seq_local, kv_local, GROUP, HD)
    new_key = joined[:, :, GROUP * HD : (GROUP + 1) * HD]
    new_value = joined[:, :, (GROUP + 1) * HD :]
    score_scale = HD ** (-0.5)
    own_score = (
        jnp.einsum("skgh,skh->skg", queries, new_key, preferred_element_type=jnp.float32)
        * score_scale
    )
    positions = jnp.arange(cache_len, dtype=jnp.int32)
    live = positions[None, None, None, :] < lengths[:, None, None, None]
    scores = (
        jnp.einsum("skgh,skth->skgt", queries, key_cache, preferred_element_type=jnp.float32)
        * score_scale
    )
    weights, own_weight = normalize(scores, own_score, live)
    mixed = jnp.einsum("skgt,skth->skgh", weights, value_cache, preferred_element_type=jnp.float32)
    mixed = (
        mixed
        + own_weight.astype(jnp.float32)[..., None] * new_value.astype(jnp.float32)[:, :, None, :]
    )
    attended = mixed.astype(jnp.bfloat16).reshape(seq_local, kv_local * GROUP * HD)
    terms = lax.dot_general(
        lax.all_gather(attended, "gy", axis=0, tiled=True),
        out_weight,
        NT,
        preferred_element_type=jnp.float32,
    )
    return lax.psum_scatter(terms.astype(jnp.bfloat16), "gx", scatter_dimension=0, tiled=True)


def swap(x):
    return lax.ppermute(x, "gx", [(0, 1), (1, 0)])


def hop(x, chips, mask):
    return lax.ppermute(x, "gy", [(chip, chip ^ mask) for chip in range(chips)])


def stage_kernel(mine_ref, out_ref):
    out_ref[...] = mine_ref[...]


def pair_kernel(mine_ref, theirs_ref, out_ref):
    out_ref[...] = jnp.concatenate([mine_ref[...], theirs_ref[...]], axis=0)


def stage(block):
    return pl.pallas_call(
        stage_kernel,
        out_shape=jax.ShapeDtypeStruct(block.shape, block.dtype),
        in_specs=in_vmem(1),
        out_specs=in_vmem(1)[0],
        compiler_params=pltpu.CompilerParams(vmem_limit_bytes=2 * MIB),
        cost_estimate=pl.CostEstimate(flops=1 << 35, bytes_accessed=1 << 17, transcendentals=0),
        name="stage",
    )(block)


def gather_rows(block, far, chips):
    pair = pl.pallas_call(
        pair_kernel,
        out_shape=jax.ShapeDtypeStruct((2 * block.shape[0], block.shape[1]), block.dtype),
        in_specs=in_vmem(2),
        out_specs=in_vmem(1)[0],
        compiler_params=pltpu.CompilerParams(vmem_limit_bytes=2 * MIB),
        name="pair",
    )(hold(block), hold(far))
    return [pair] + [hop(pair, chips, mask) for mask in range(1, chips // 2)]


def project_kernel(*refs, swapped):
    *x_refs, w_ref, out_ref = refs
    heads = out_ref.shape[0]
    x = jnp.concatenate([x_ref[...] for x_ref in x_refs], axis=0)
    core = lax.axis_index("gx")
    first = heads * ((1 - core) if swapped else core)
    for head in range(heads):
        value = lax.dot_general(x, w_ref[first + head], NT, preferred_element_type=jnp.float32)
        out_ref[head] = value.astype(jnp.bfloat16)


def attend_kernel(lengths_ref, got_ref, key_ref, value_ref, out_ref, wide, tall, flat):
    half = got_ref.shape[0]
    seqs, heads, slots = key_ref.shape[0], key_ref.shape[1], key_ref.shape[2]
    part = got_ref.shape[4]
    chip = lax.axis_index("gy")
    for head in range(heads):
        for other in range(2 * half):
            mask = chip ^ other
            piece = got_ref[mask & (half - 1), mask // half, head]
            wide[:, other * part : (other + 1) * part] = piece.astype(jnp.float32)
        for column in range(GROUP + 2):
            tall[head, :, column, :] = wide[:, column * HD : (column + 1) * HD]
    scale = HD ** (-0.5)
    position = lax.broadcasted_iota(jnp.int32, (GROUP, slots), 1)
    for seq in range(seqs):
        live = position < lengths_ref[seq]
        for head in range(heads):
            query = tall[head, seq, :GROUP, :]
            new_key = tall[head, seq, GROUP : GROUP + 1, :]
            new_value = tall[head, seq, GROUP + 1 : GROUP + 2, :]
            own = jnp.sum(query * new_key, axis=1, keepdims=True) * scale
            scores = lax.dot_general(
                query.astype(jnp.bfloat16), key_ref[seq, head], NT, preferred_element_type=jnp.float32
            )
            scores = jnp.where(live, scores * scale, NEG_FILL)
            top = jnp.maximum(jnp.max(scores, axis=1, keepdims=True), own)
            weights = jnp.where(live, jnp.exp(scores - top), 0.0)
            own_weight = jnp.exp(own - top)
            denom = jnp.sum(weights, axis=1, keepdims=True) + own_weight
            weights = (weights / denom).astype(jnp.bfloat16)
            own_weight = (own_weight / denom).astype(jnp.bfloat16).astype(jnp.float32)
            mixed = jnp.dot(weights, value_ref[seq, head], preferred_element_type=jnp.float32)
            mixed = mixed + own_weight * new_value
            for query_head in range(GROUP):
                column = (head * GROUP + query_head) * HD
                flat[seq : seq + 1, column : column + HD] = mixed[query_head : query_head + 1]
    out_ref[...] = flat[...].astype(jnp.bfloat16)


def output_kernel(*refs, rows):
    *x_refs, w_ref, keep_ref, send_ref = refs
    x = jnp.concatenate([x_ref[...] for x_ref in x_refs], axis=0)
    total = x.shape[0]
    half = len(x_refs)
    chip, core = lax.axis_index("gy"), lax.axis_index("gx")
    row = lax.broadcasted_iota(jnp.int32, (total, total), 0)
    column = lax.broadcasted_iota(jnp.int32, (total, total), 1)
    side, within = row // (half * rows), row % (half * rows)
    mask = chip ^ ((core ^ side) * half + within // rows)
    source = (mask % half) * (2 * rows) + (mask // half) * rows + within % rows
    order = jnp.where(column == source, 1.0, 0.0).astype(jnp.bfloat16)
    x = jnp.dot(order, x, preferred_element_type=jnp.float32).astype(jnp.bfloat16)
    value = lax.dot_general(x, w_ref[...], NT, preferred_element_type=jnp.float32)
    value = value.astype(jnp.bfloat16)
    keep_ref[...] = value[: half * rows]
    send_ref[...] = value[half * rows :]


def in_vmem(count):
    return [pl.BlockSpec(memory_space=pltpu.VMEM)] * count


def hold(x):
    return pltpu.with_memory_space_constraint(x, pltpu.VMEM)


def local(activations, qkv_weight, out_weight, key_cache, value_cache, lengths, *, chips):
    _, part, width = qkv_weight.shape
    seqs, kv_local, slots, _ = key_cache.shape
    out_cols, feats = out_weight.shape
    half = chips // 2
    rows = chips * seqs
    limits = pltpu.CompilerParams(vmem_limit_bytes=8 * MIB)
    qkv_weight, out_weight = hold(qkv_weight), hold(out_weight)
    key_cache, value_cache = hold(key_cache), hold(value_cache)

    pieces = [hold(piece) for piece in gather_rows(stage(activations), hop(activations, chips, half), chips)]

    def project(swapped):
        return pl.pallas_call(
            functools.partial(project_kernel, swapped=swapped),
            out_shape=jax.ShapeDtypeStruct((kv_local, rows, part), jnp.bfloat16),
            in_specs=in_vmem(half + 1),
            out_specs=in_vmem(1)[0],
            compiler_params=limits,
            cost_estimate=pl.CostEstimate(
                flops=2 * kv_local * 256 * part * width, bytes_accessed=1 << 20, transcendentals=0
            ),
            name="project",
        )(*pieces, qkv_weight)

    arrived = swap(project(True))
    joined = (project(False).astype(jnp.float32) + arrived.astype(jnp.float32)).astype(jnp.bfloat16)
    joined = joined.reshape(kv_local, half, 2, seqs, part)
    near = [joined[:, mask, 0] for mask in range(half)]
    far = hop(jnp.stack([joined[:, mask, 1] for mask in range(half)]), chips, half)
    got = [jnp.stack([near[mask], far[mask]]) for mask in range(half)]
    got = [got[0]] + [hop(got[mask], chips, mask) for mask in range(1, half)]

    attended = pl.pallas_call(
        attend_kernel,
        out_shape=jax.ShapeDtypeStruct((seqs, feats), jnp.bfloat16),
        in_specs=[pl.BlockSpec(memory_space=pltpu.SMEM)] + in_vmem(3),
        out_specs=in_vmem(1)[0],
        scratch_shapes=[
            pltpu.VMEM((seqs, chips * part), jnp.float32),
            pltpu.VMEM((kv_local, seqs, GROUP + 8, HD), jnp.float32),
            pltpu.VMEM((seqs, feats), jnp.float32),
        ],
        compiler_params=limits,
        name="attend",
    )(lengths, hold(jnp.stack(got)), key_cache, value_cache)

    pieces = [hold(piece) for piece in gather_rows(attended, hop(attended, chips, half), chips)]
    piece = jax.ShapeDtypeStruct((rows // 2, out_cols), jnp.bfloat16)
    keep, send = pl.pallas_call(
        functools.partial(output_kernel, rows=seqs),
        out_shape=(piece, piece),
        in_specs=in_vmem(half + 1),
        out_specs=tuple(in_vmem(2)),
        compiler_params=limits,
        name="output",
    )(*pieces, out_weight)
    return (keep.astype(jnp.float32) + swap(send).astype(jnp.float32)).astype(jnp.bfloat16)


def solution(mesh):
    in_specs = (
        P(("parts", "gy"), "gx"),
        P(None, "gy", "gx"),
        P("gy", "gx"),
        P(("parts", "gy"), "gx", None, None),
        P(("parts", "gy"), "gx", None, None),
        P(("parts", "gy")),
    )
    out_specs = P(("parts", "gx"), "gy")
    chips = mesh.shape["gy"]

    def whole(activations, qkv_weight, *rest):
        part = qkv_weight.shape[1] // chips
        seqs = activations.shape[0] // (mesh.shape["parts"] * chips)
        paired = mesh.shape["gx"] == 2 and chips in (2, 4, 8, 16) and part % 16 == 0
        paired = paired and seqs & (seqs - 1) == 0 and (chips // 2 * seqs) % 16 == 0
        body = functools.partial(local, chips=chips) if paired else local_plain
        return jax.shard_map(
            body, mesh=mesh, in_specs=in_specs, out_specs=out_specs, check_vma=False
        )(activations, qkv_weight, *rest)

    return whole
```

```python
import functools

import jax
import jax.numpy as jnp
from jax import lax
from jax.experimental import pallas as pl
from jax.experimental.pallas import tpu as pltpu
from jax.sharding import PartitionSpec as P

HD = 128
GROUP = 16
MIB = 1 << 20
NEG_FILL = -1e30
NT = (((1,), (1,)), ((), ()))


def normalize(scores, own_score, live):
    scores = jnp.where(live, scores, NEG_FILL)
    top = jnp.maximum(jnp.max(scores, axis=3), own_score)
    weights = jnp.where(live, jnp.exp(scores - top[..., None]), 0.0)
    own_weight = jnp.exp(own_score - top)
    denom = jnp.sum(weights, axis=3) + own_weight
    return (
        (weights / denom[..., None]).astype(jnp.bfloat16),
        (own_weight / denom).astype(jnp.bfloat16),
    )


def local_plain(activations, qkv_weight, out_weight, key_cache, value_cache, lengths):
    head_count, col_part, half_width = qkv_weight.shape
    flat_weight = qkv_weight.reshape(head_count * col_part, half_width)
    row_piece = lax.all_gather(activations, "gy", axis=0, tiled=True)
    product = lax.dot_general(row_piece, flat_weight, NT, preferred_element_type=jnp.float32)
    partial_value = product.reshape(row_piece.shape[0], head_count, col_part)
    summed = lax.psum_scatter(
        partial_value.astype(jnp.bfloat16), "gx", scatter_dimension=1, tiled=True
    )
    joined = lax.all_to_all(summed, "gy", split_axis=0, concat_axis=2, tiled=True)
    seq_local, kv_local, cache_len = (key_cache.shape[0], key_cache.shape[1], key_cache.shape[2])
    queries = joined[:, :, : GROUP * HD].reshape(seq_local, kv_local, GROUP, HD)
    new_key = joined[:, :, GROUP * HD : (GROUP + 1) * HD]
    new_value = joined[:, :, (GROUP + 1) * HD :]
    score_scale = HD ** (-0.5)
    own_score = (
        jnp.einsum("skgh,skh->skg", queries, new_key, preferred_element_type=jnp.float32)
        * score_scale
    )
    positions = jnp.arange(cache_len, dtype=jnp.int32)
    live = positions[None, None, None, :] < lengths[:, None, None, None]
    scores = (
        jnp.einsum("skgh,skth->skgt", queries, key_cache, preferred_element_type=jnp.float32)
        * score_scale
    )
    weights, own_weight = normalize(scores, own_score, live)
    mixed = jnp.einsum("skgt,skth->skgh", weights, value_cache, preferred_element_type=jnp.float32)
    mixed = (
        mixed
        + own_weight.astype(jnp.float32)[..., None] * new_value.astype(jnp.float32)[:, :, None, :]
    )
    attended = mixed.astype(jnp.bfloat16).reshape(seq_local, kv_local * GROUP * HD)
    terms = lax.dot_general(
        lax.all_gather(attended, "gy", axis=0, tiled=True),
        out_weight,
        NT,
        preferred_element_type=jnp.float32,
    )
    return lax.psum_scatter(terms.astype(jnp.bfloat16), "gx", scatter_dimension=0, tiled=True)


def swap(x):
    return lax.ppermute(x, "gx", [(0, 1), (1, 0)])


def hop(x, chips, mask):
    return lax.ppermute(x, "gy", [(chip, chip ^ mask) for chip in range(chips)])


def stage_kernel(mine_ref, out_ref):
    out_ref[...] = mine_ref[...]


def pair_kernel(mine_ref, theirs_ref, out_ref):
    out_ref[...] = jnp.concatenate([mine_ref[...], theirs_ref[...]], axis=0)


def stage(block):
    return pl.pallas_call(
        stage_kernel,
        out_shape=jax.ShapeDtypeStruct(block.shape, block.dtype),
        in_specs=in_vmem(1),
        out_specs=in_vmem(1)[0],
        compiler_params=pltpu.CompilerParams(vmem_limit_bytes=2 * MIB),
        cost_estimate=pl.CostEstimate(flops=1 << 35, bytes_accessed=1 << 17, transcendentals=0),
        name="stage",
    )(block)


def gather_rows(block, far, chips):
    pair = pl.pallas_call(
        pair_kernel,
        out_shape=jax.ShapeDtypeStruct((2 * block.shape[0], block.shape[1]), block.dtype),
        in_specs=in_vmem(2),
        out_specs=in_vmem(1)[0],
        compiler_params=pltpu.CompilerParams(vmem_limit_bytes=2 * MIB),
        name="pair",
    )(hold(block), hold(far))
    return [pair] + [hop(pair, chips, mask) for mask in range(1, chips // 2)]


def project_kernel(*refs, swapped):
    *x_refs, w_ref, out_ref = refs
    heads = out_ref.shape[0]
    x = jnp.concatenate([x_ref[...] for x_ref in x_refs], axis=0)
    core = lax.axis_index("gx")
    first = heads * ((1 - core) if swapped else core)
    for head in range(heads):
        value = lax.dot_general(x, w_ref[first + head], NT, preferred_element_type=jnp.float32)
        out_ref[head] = value.astype(jnp.bfloat16)


def merge_kernel(near_ref, far_ref, *out_refs):
    for mask, out_ref in enumerate(reversed(out_refs)):
        out_ref[0] = near_ref[mask]
        out_ref[1] = far_ref[mask]


def attend_kernel(lengths_ref, *refs):
    *got_refs, key_ref, value_ref, out_ref, got, wide, tall, flat = refs
    half = len(got_refs)
    seqs, heads, slots = key_ref.shape[0], key_ref.shape[1], key_ref.shape[2]
    part = got.shape[4]
    chip = lax.axis_index("gy")
    for mask, got_ref in enumerate(reversed(got_refs)):
        got[mask] = got_ref[...]
    for other in range(2 * half):
        mask = chip ^ other
        piece = got[mask & (half - 1), mask // half]
        wide[:, :, other * part : (other + 1) * part] = piece.astype(jnp.float32)
    for column in range(GROUP + 2):
        for head in range(heads):
            tall[:, head, column, :] = wide[head, :, column * HD : (column + 1) * HD]
    scale = HD ** (-0.5)
    pairs = [(seq, head) for seq in range(seqs) for head in range(heads)]
    position = lax.broadcasted_iota(jnp.int32, (GROUP, slots), 1)
    queries, own, scores, live = [], [], [], []
    for seq, head in pairs:
        query = tall[seq, head, :GROUP, :]
        new_key = tall[seq, head, GROUP : GROUP + 1, :]
        own.append(jnp.sum(query * new_key, axis=1, keepdims=True))
        scores.append(
            lax.dot_general(
                query.astype(jnp.bfloat16), key_ref[seq, head], NT, preferred_element_type=jnp.float32
            )
        )
        live.append(jnp.where(position < lengths_ref[seq], 1.0, 0.0))
    live = jnp.concatenate(live, axis=0) > 0.5
    own = jnp.concatenate(own, axis=0) * scale
    scores = jnp.where(live, jnp.concatenate(scores, axis=0) * scale, NEG_FILL)
    top = jnp.maximum(jnp.max(scores, axis=1, keepdims=True), own)
    weights = jnp.where(live, jnp.exp(scores - top), 0.0)
    own_weight = jnp.exp(own - top)
    share = 1.0 / (jnp.sum(weights, axis=1, keepdims=True) + own_weight)
    weights = (weights * share).astype(jnp.bfloat16)
    own_weight = (own_weight * share).astype(jnp.bfloat16).astype(jnp.float32)
    for at, (seq, head) in enumerate(pairs):
        rows = slice(at * GROUP, (at + 1) * GROUP)
        mixed = jnp.dot(weights[rows], value_ref[seq, head], preferred_element_type=jnp.float32)
        mixed = mixed + own_weight[rows] * tall[seq, head, GROUP + 1 : GROUP + 2, :]
        for query_head in range(GROUP):
            column = (head * GROUP + query_head) * HD
            flat[seq : seq + 1, column : column + HD] = mixed[query_head : query_head + 1]
    out_ref[...] = flat[...].astype(jnp.bfloat16)


def output_kernel(*refs, rows):
    *x_refs, w_ref, keep_ref, send_ref = refs
    x = jnp.concatenate([x_ref[...] for x_ref in x_refs], axis=0)
    total = x.shape[0]
    half = len(x_refs)
    chip, core = lax.axis_index("gy"), lax.axis_index("gx")
    row = lax.broadcasted_iota(jnp.int32, (total, total), 0)
    column = lax.broadcasted_iota(jnp.int32, (total, total), 1)
    side, within = row // (half * rows), row % (half * rows)
    mask = chip ^ ((core ^ side) * half + within // rows)
    source = (mask % half) * (2 * rows) + (mask // half) * rows + within % rows
    order = jnp.where(column == source, 1.0, 0.0).astype(jnp.bfloat16)
    x = jnp.dot(order, x, preferred_element_type=jnp.float32).astype(jnp.bfloat16)
    value = lax.dot_general(x, w_ref[...], NT, preferred_element_type=jnp.float32)
    value = value.astype(jnp.bfloat16)
    keep_ref[...] = value[: half * rows]
    send_ref[...] = value[half * rows :]


def in_vmem(count):
    return [pl.BlockSpec(memory_space=pltpu.VMEM)] * count


def hold(x):
    return pltpu.with_memory_space_constraint(x, pltpu.VMEM)


def local(activations, qkv_weight, out_weight, key_cache, value_cache, lengths, *, chips):
    _, part, width = qkv_weight.shape
    seqs, kv_local, slots, _ = key_cache.shape
    out_cols, feats = out_weight.shape
    half = chips // 2
    rows = chips * seqs
    limits = pltpu.CompilerParams(vmem_limit_bytes=8 * MIB)
    qkv_weight, out_weight = hold(qkv_weight), hold(out_weight)
    key_cache, value_cache = hold(key_cache), hold(value_cache)

    pieces = [hold(piece) for piece in gather_rows(stage(activations), hop(activations, chips, half), chips)]

    def project(swapped):
        return pl.pallas_call(
            functools.partial(project_kernel, swapped=swapped),
            out_shape=jax.ShapeDtypeStruct((kv_local, rows, part), jnp.bfloat16),
            in_specs=in_vmem(half + 1),
            out_specs=in_vmem(1)[0],
            compiler_params=limits,
            cost_estimate=pl.CostEstimate(
                flops=2 * kv_local * 256 * part * width, bytes_accessed=1 << 20, transcendentals=0
            ),
            name="project",
        )(*pieces, qkv_weight)

    arrived = swap(project(True))
    joined = (project(False).astype(jnp.float32) + arrived.astype(jnp.float32)).astype(jnp.bfloat16)
    joined = joined.reshape(kv_local, half, 2, seqs, part)
    near = jnp.stack([joined[:, mask, 0] for mask in range(half)])
    far = hop(jnp.stack([joined[:, mask, 1] for mask in range(half)]), chips, half)
    *far_first, mine = pl.pallas_call(
        merge_kernel,
        out_shape=(jax.ShapeDtypeStruct((2, kv_local, seqs, part), jnp.bfloat16),) * half,
        in_specs=in_vmem(2),
        out_specs=tuple(in_vmem(half)),
        compiler_params=pltpu.CompilerParams(vmem_limit_bytes=2 * MIB),
        name="merge",
    )(hold(near), hold(far))
    got = [hop(piece, chips, half - 1 - at) for at, piece in enumerate(far_first)] + [mine]

    attended = pl.pallas_call(
        attend_kernel,
        out_shape=jax.ShapeDtypeStruct((seqs, feats), jnp.bfloat16),
        in_specs=[pl.BlockSpec(memory_space=pltpu.SMEM)] + in_vmem(half + 2),
        out_specs=in_vmem(1)[0],
        scratch_shapes=[
            pltpu.VMEM((half, 2, kv_local, seqs, part), jnp.bfloat16),
            pltpu.VMEM((kv_local, seqs, chips * part), jnp.float32),
            pltpu.VMEM((seqs, kv_local, GROUP + 8, HD), jnp.float32),
            pltpu.VMEM((seqs, feats), jnp.float32),
        ],
        compiler_params=limits,
        name="attend",
    )(lengths, *[hold(piece) for piece in got], key_cache, value_cache)

    pieces = [hold(piece) for piece in gather_rows(attended, hop(attended, chips, half), chips)]
    piece = jax.ShapeDtypeStruct((rows // 2, out_cols), jnp.bfloat16)
    keep, send = pl.pallas_call(
        functools.partial(output_kernel, rows=seqs),
        out_shape=(piece, piece),
        in_specs=in_vmem(half + 1),
        out_specs=tuple(in_vmem(2)),
        compiler_params=limits,
        name="output",
    )(*pieces, out_weight)
    return (keep.astype(jnp.float32) + swap(send).astype(jnp.float32)).astype(jnp.bfloat16)


def solution(mesh):
    in_specs = (
        P(("parts", "gy"), "gx"),
        P(None, "gy", "gx"),
        P("gy", "gx"),
        P(("parts", "gy"), "gx", None, None),
        P(("parts", "gy"), "gx", None, None),
        P(("parts", "gy")),
    )
    out_specs = P(("parts", "gx"), "gy")
    chips = mesh.shape["gy"]

    def whole(activations, qkv_weight, *rest):
        part = qkv_weight.shape[1] // chips
        seqs = activations.shape[0] // (mesh.shape["parts"] * chips)
        paired = mesh.shape["gx"] == 2 and chips in (2, 4, 8, 16) and part % 16 == 0
        paired = paired and seqs & (seqs - 1) == 0 and (chips // 2 * seqs) % 16 == 0
        body = functools.partial(local, chips=chips) if paired else local_plain
        return jax.shard_map(
            body, mesh=mesh, in_specs=in_specs, out_specs=out_specs, check_vma=False
        )(activations, qkv_weight, *rest)

    return whole
```

```python
import functools

import jax
import jax.numpy as jnp
from jax import lax
from jax.experimental import pallas as pl
from jax.experimental.pallas import tpu as pltpu
from jax.sharding import PartitionSpec as P

HD = 128
GROUP = 16
MIB = 1 << 20
NEG_FILL = -1e30
NT = (((1,), (1,)), ((), ()))


def normalize(scores, own_score, live):
    scores = jnp.where(live, scores, NEG_FILL)
    top = jnp.maximum(jnp.max(scores, axis=3), own_score)
    weights = jnp.where(live, jnp.exp(scores - top[..., None]), 0.0)
    own_weight = jnp.exp(own_score - top)
    denom = jnp.sum(weights, axis=3) + own_weight
    return (
        (weights / denom[..., None]).astype(jnp.bfloat16),
        (own_weight / denom).astype(jnp.bfloat16),
    )


def local_plain(activations, qkv_weight, out_weight, key_cache, value_cache, lengths):
    head_count, col_part, half_width = qkv_weight.shape
    flat_weight = qkv_weight.reshape(head_count * col_part, half_width)
    row_piece = lax.all_gather(activations, "gy", axis=0, tiled=True)
    product = lax.dot_general(row_piece, flat_weight, NT, preferred_element_type=jnp.float32)
    partial_value = product.reshape(row_piece.shape[0], head_count, col_part)
    summed = lax.psum_scatter(
        partial_value.astype(jnp.bfloat16), "gx", scatter_dimension=1, tiled=True
    )
    joined = lax.all_to_all(summed, "gy", split_axis=0, concat_axis=2, tiled=True)
    seq_local, kv_local, cache_len = (key_cache.shape[0], key_cache.shape[1], key_cache.shape[2])
    queries = joined[:, :, : GROUP * HD].reshape(seq_local, kv_local, GROUP, HD)
    new_key = joined[:, :, GROUP * HD : (GROUP + 1) * HD]
    new_value = joined[:, :, (GROUP + 1) * HD :]
    score_scale = HD ** (-0.5)
    own_score = (
        jnp.einsum("skgh,skh->skg", queries, new_key, preferred_element_type=jnp.float32)
        * score_scale
    )
    positions = jnp.arange(cache_len, dtype=jnp.int32)
    live = positions[None, None, None, :] < lengths[:, None, None, None]
    scores = (
        jnp.einsum("skgh,skth->skgt", queries, key_cache, preferred_element_type=jnp.float32)
        * score_scale
    )
    weights, own_weight = normalize(scores, own_score, live)
    mixed = jnp.einsum("skgt,skth->skgh", weights, value_cache, preferred_element_type=jnp.float32)
    mixed = (
        mixed
        + own_weight.astype(jnp.float32)[..., None] * new_value.astype(jnp.float32)[:, :, None, :]
    )
    attended = mixed.astype(jnp.bfloat16).reshape(seq_local, kv_local * GROUP * HD)
    terms = lax.dot_general(
        lax.all_gather(attended, "gy", axis=0, tiled=True),
        out_weight,
        NT,
        preferred_element_type=jnp.float32,
    )
    return lax.psum_scatter(terms.astype(jnp.bfloat16), "gx", scatter_dimension=0, tiled=True)


def swap(x):
    return lax.ppermute(x, "gx", [(0, 1), (1, 0)])


def hop(x, chips, mask):
    return lax.ppermute(x, "gy", [(chip, chip ^ mask) for chip in range(chips)])


def stage_kernel(mine_ref, out_ref):
    out_ref[...] = mine_ref[...]


def pair_kernel(mine_ref, theirs_ref, out_ref):
    out_ref[...] = jnp.concatenate([mine_ref[...], theirs_ref[...]], axis=0)


def stage(block):
    return pl.pallas_call(
        stage_kernel,
        out_shape=jax.ShapeDtypeStruct(block.shape, block.dtype),
        in_specs=in_vmem(1),
        out_specs=in_vmem(1)[0],
        compiler_params=pltpu.CompilerParams(vmem_limit_bytes=2 * MIB),
        cost_estimate=pl.CostEstimate(flops=1 << 35, bytes_accessed=1 << 17, transcendentals=0),
        name="stage",
    )(block)


def gather_rows(block, far, chips):
    pair = pl.pallas_call(
        pair_kernel,
        out_shape=jax.ShapeDtypeStruct((2 * block.shape[0], block.shape[1]), block.dtype),
        in_specs=in_vmem(2),
        out_specs=in_vmem(1)[0],
        compiler_params=pltpu.CompilerParams(vmem_limit_bytes=2 * MIB),
        name="pair",
    )(hold(block), hold(far))
    return [pair] + [hop(pair, chips, mask) for mask in range(1, chips // 2)]


def gather_early(block, staged, chips):
    half = chips // 2
    far = hop(block, chips, half)
    masks = range(half - 1, 0, -1)
    near = {mask: hop(block, chips, mask) for mask in masks}
    beyond = {mask: hop(far, chips, mask) for mask in masks}
    pieces = [staged, far]
    for mask in range(1, half):
        pieces += [near[mask], beyond[mask]]
    return pieces


def project_kernel(*refs, swapped):
    *x_refs, w_ref, out_ref = refs
    heads = out_ref.shape[0]
    x = jnp.concatenate([x_ref[...] for x_ref in x_refs], axis=0)
    core = lax.axis_index("gx")
    first = heads * ((1 - core) if swapped else core)
    for head in range(heads):
        value = lax.dot_general(w_ref[first + head], x, NT, preferred_element_type=jnp.float32)
        out_ref[head] = value.T.astype(jnp.bfloat16)


def merge_kernel(near_ref, far_ref, *out_refs):
    for mask, out_ref in enumerate(reversed(out_refs)):
        out_ref[0] = near_ref[mask]
        out_ref[1] = far_ref[mask]


def attend_kernel(lengths_ref, *refs):
    *got_refs, key_ref, value_ref, out_ref, got, wide, tall, flat = refs
    half = len(got_refs)
    seqs, heads, slots = key_ref.shape[0], key_ref.shape[1], key_ref.shape[2]
    part = got.shape[4]
    chip = lax.axis_index("gy")
    for mask, got_ref in enumerate(reversed(got_refs)):
        got[mask] = got_ref[...]
    for other in range(2 * half):
        mask = chip ^ other
        piece = got[mask & (half - 1), mask // half]
        wide[:, :, other * part : (other + 1) * part] = piece.astype(jnp.float32)
    for column in range(GROUP + 2):
        for head in range(heads):
            tall[:, head, column, :] = wide[head, :, column * HD : (column + 1) * HD]
    scale = HD ** (-0.5)
    pairs = [(seq, head) for seq in range(seqs) for head in range(heads)]
    position = lax.broadcasted_iota(jnp.int32, (GROUP, slots), 1)
    queries, own, scores, live = [], [], [], []
    for seq, head in pairs:
        query = tall[seq, head, :GROUP, :]
        new_key = tall[seq, head, GROUP : GROUP + 1, :]
        own.append(jnp.sum(query * new_key, axis=1, keepdims=True))
        scores.append(
            lax.dot_general(
                query.astype(jnp.bfloat16), key_ref[seq, head], NT, preferred_element_type=jnp.float32
            )
        )
        live.append(jnp.where(position < lengths_ref[seq], 1.0, 0.0))
    live = jnp.concatenate(live, axis=0) > 0.5
    own = jnp.concatenate(own, axis=0) * scale
    scores = jnp.where(live, jnp.concatenate(scores, axis=0) * scale, NEG_FILL)
    top = jnp.maximum(jnp.max(scores, axis=1, keepdims=True), own)
    weights = jnp.where(live, jnp.exp(scores - top), 0.0)
    own_weight = jnp.exp(own - top)
    share = 1.0 / (jnp.sum(weights, axis=1, keepdims=True) + own_weight)
    weights = (weights * share).astype(jnp.bfloat16)
    own_weight = (own_weight * share).astype(jnp.bfloat16).astype(jnp.float32)
    for at, (seq, head) in enumerate(pairs):
        rows = slice(at * GROUP, (at + 1) * GROUP)
        mixed = jnp.dot(weights[rows], value_ref[seq, head], preferred_element_type=jnp.float32)
        mixed = mixed + own_weight[rows] * tall[seq, head, GROUP + 1 : GROUP + 2, :]
        for query_head in range(GROUP):
            column = (head * GROUP + query_head) * HD
            flat[seq : seq + 1, column : column + HD] = mixed[query_head : query_head + 1]
    out_ref[...] = flat[...].astype(jnp.bfloat16)


def output_kernel(*refs, rows):
    *x_refs, w_ref, keep_ref, send_ref = refs
    x = jnp.concatenate([x_ref[...] for x_ref in x_refs], axis=0)
    total = x.shape[0]
    half = len(x_refs)
    chip, core = lax.axis_index("gy"), lax.axis_index("gx")
    row = lax.broadcasted_iota(jnp.int32, (total, total), 0)
    column = lax.broadcasted_iota(jnp.int32, (total, total), 1)
    side, within = row // (half * rows), row % (half * rows)
    mask = chip ^ ((core ^ side) * half + within // rows)
    source = (mask % half) * (2 * rows) + (mask // half) * rows + within % rows
    order = jnp.where(column == source, 1.0, 0.0).astype(jnp.bfloat16)
    x = jnp.dot(order, x, preferred_element_type=jnp.float32).astype(jnp.bfloat16)
    cols = w_ref.shape[0]
    width = min(cols, 256)
    for at in range(0, cols, width):
        value = lax.dot_general(w_ref[at : at + width], x, NT, preferred_element_type=jnp.float32)
        value = value.T.astype(jnp.bfloat16)
        keep_ref[:, at : at + width] = value[: half * rows]
        send_ref[:, at : at + width] = value[half * rows :]


def in_vmem(count):
    return [pl.BlockSpec(memory_space=pltpu.VMEM)] * count


def hold(x):
    return pltpu.with_memory_space_constraint(x, pltpu.VMEM)


def local(activations, qkv_weight, out_weight, key_cache, value_cache, lengths, *, chips):
    _, part, width = qkv_weight.shape
    seqs, kv_local, slots, _ = key_cache.shape
    out_cols, feats = out_weight.shape
    half = chips // 2
    rows = chips * seqs
    limits = pltpu.CompilerParams(vmem_limit_bytes=8 * MIB)
    qkv_weight, out_weight = hold(qkv_weight), hold(out_weight)
    key_cache, value_cache = hold(key_cache), hold(value_cache)

    pieces = [hold(piece) for piece in gather_early(activations, stage(activations), chips)]

    def project(swapped):
        return pl.pallas_call(
            functools.partial(project_kernel, swapped=swapped),
            out_shape=jax.ShapeDtypeStruct((kv_local, rows, part), jnp.bfloat16),
            in_specs=in_vmem(chips + 1),
            out_specs=in_vmem(1)[0],
            compiler_params=limits,
            cost_estimate=pl.CostEstimate(
                flops=2 * kv_local * 256 * part * width, bytes_accessed=1 << 20, transcendentals=0
            ),
            name="project",
        )(*pieces, qkv_weight)

    arrived = swap(project(True))
    joined = (project(False).astype(jnp.float32) + arrived.astype(jnp.float32)).astype(jnp.bfloat16)
    joined = joined.reshape(kv_local, half, 2, seqs, part)
    near = jnp.stack([joined[:, mask, 0] for mask in range(half)])
    far = hop(jnp.stack([joined[:, mask, 1] for mask in range(half)]), chips, half)
    *far_first, mine = pl.pallas_call(
        merge_kernel,
        out_shape=(jax.ShapeDtypeStruct((2, kv_local, seqs, part), jnp.bfloat16),) * half,
        in_specs=in_vmem(2),
        out_specs=tuple(in_vmem(half)),
        compiler_params=pltpu.CompilerParams(vmem_limit_bytes=2 * MIB),
        name="merge",
    )(hold(near), hold(far))
    got = [hop(piece, chips, half - 1 - at) for at, piece in enumerate(far_first)] + [mine]

    attended = pl.pallas_call(
        attend_kernel,
        out_shape=jax.ShapeDtypeStruct((seqs, feats), jnp.bfloat16),
        in_specs=[pl.BlockSpec(memory_space=pltpu.SMEM)] + in_vmem(half + 2),
        out_specs=in_vmem(1)[0],
        scratch_shapes=[
            pltpu.VMEM((half, 2, kv_local, seqs, part), jnp.bfloat16),
            pltpu.VMEM((kv_local, seqs, chips * part), jnp.float32),
            pltpu.VMEM((seqs, kv_local, GROUP + 8, HD), jnp.float32),
            pltpu.VMEM((seqs, feats), jnp.float32),
        ],
        compiler_params=limits,
        name="attend",
    )(lengths, *[hold(piece) for piece in got], key_cache, value_cache)

    pieces = [hold(piece) for piece in gather_rows(attended, hop(attended, chips, half), chips)]
    piece = jax.ShapeDtypeStruct((rows // 2, out_cols), jnp.bfloat16)
    keep, send = pl.pallas_call(
        functools.partial(output_kernel, rows=seqs),
        out_shape=(piece, piece),
        in_specs=in_vmem(half + 1),
        out_specs=tuple(in_vmem(2)),
        compiler_params=limits,
        name="output",
    )(*pieces, out_weight)
    return (keep.astype(jnp.float32) + swap(send).astype(jnp.float32)).astype(jnp.bfloat16)


def solution(mesh):
    in_specs = (
        P(("parts", "gy"), "gx"),
        P(None, "gy", "gx"),
        P("gy", "gx"),
        P(("parts", "gy"), "gx", None, None),
        P(("parts", "gy"), "gx", None, None),
        P(("parts", "gy")),
    )
    out_specs = P(("parts", "gx"), "gy")
    chips = mesh.shape["gy"]

    def whole(activations, qkv_weight, *rest):
        part = qkv_weight.shape[1] // chips
        seqs = activations.shape[0] // (mesh.shape["parts"] * chips)
        paired = mesh.shape["gx"] == 2 and chips in (2, 4, 8, 16) and part % 16 == 0
        paired = paired and seqs & (seqs - 1) == 0 and (chips // 2 * seqs) % 16 == 0
        body = functools.partial(local, chips=chips) if paired else local_plain
        return jax.shard_map(
            body, mesh=mesh, in_specs=in_specs, out_specs=out_specs, check_vma=False
        )(activations, qkv_weight, *rest)

    return whole
```

```python
import functools

import jax
import jax.numpy as jnp
from jax import lax
from jax.experimental import pallas as pl
from jax.experimental.pallas import tpu as pltpu
from jax.sharding import PartitionSpec as P

HD = 128
GROUP = 16
MIB = 1 << 20
NEG_FILL = -1e30
NT = (((1,), (1,)), ((), ()))


def normalize(scores, own_score, live):
    scores = jnp.where(live, scores, NEG_FILL)
    top = jnp.maximum(jnp.max(scores, axis=3), own_score)
    weights = jnp.where(live, jnp.exp(scores - top[..., None]), 0.0)
    own_weight = jnp.exp(own_score - top)
    denom = jnp.sum(weights, axis=3) + own_weight
    return (
        (weights / denom[..., None]).astype(jnp.bfloat16),
        (own_weight / denom).astype(jnp.bfloat16),
    )


def local_plain(activations, qkv_weight, out_weight, key_cache, value_cache, lengths):
    head_count, col_part, half_width = qkv_weight.shape
    flat_weight = qkv_weight.reshape(head_count * col_part, half_width)
    row_piece = lax.all_gather(activations, "gy", axis=0, tiled=True)
    product = lax.dot_general(row_piece, flat_weight, NT, preferred_element_type=jnp.float32)
    partial_value = product.reshape(row_piece.shape[0], head_count, col_part)
    summed = lax.psum_scatter(
        partial_value.astype(jnp.bfloat16), "gx", scatter_dimension=1, tiled=True
    )
    joined = lax.all_to_all(summed, "gy", split_axis=0, concat_axis=2, tiled=True)
    seq_local, kv_local, cache_len = (key_cache.shape[0], key_cache.shape[1], key_cache.shape[2])
    queries = joined[:, :, : GROUP * HD].reshape(seq_local, kv_local, GROUP, HD)
    new_key = joined[:, :, GROUP * HD : (GROUP + 1) * HD]
    new_value = joined[:, :, (GROUP + 1) * HD :]
    score_scale = HD ** (-0.5)
    own_score = (
        jnp.einsum("skgh,skh->skg", queries, new_key, preferred_element_type=jnp.float32)
        * score_scale
    )
    positions = jnp.arange(cache_len, dtype=jnp.int32)
    live = positions[None, None, None, :] < lengths[:, None, None, None]
    scores = (
        jnp.einsum("skgh,skth->skgt", queries, key_cache, preferred_element_type=jnp.float32)
        * score_scale
    )
    weights, own_weight = normalize(scores, own_score, live)
    mixed = jnp.einsum("skgt,skth->skgh", weights, value_cache, preferred_element_type=jnp.float32)
    mixed = (
        mixed
        + own_weight.astype(jnp.float32)[..., None] * new_value.astype(jnp.float32)[:, :, None, :]
    )
    attended = mixed.astype(jnp.bfloat16).reshape(seq_local, kv_local * GROUP * HD)
    terms = lax.dot_general(
        lax.all_gather(attended, "gy", axis=0, tiled=True),
        out_weight,
        NT,
        preferred_element_type=jnp.float32,
    )
    return lax.psum_scatter(terms.astype(jnp.bfloat16), "gx", scatter_dimension=0, tiled=True)


def swap(x):
    return lax.ppermute(x, "gx", [(0, 1), (1, 0)])


def hop(x, chips, mask):
    pairs = [(2 * g + c, 2 * (g ^ mask) + 1 - c) for g in range(chips) for c in range(2)]
    return lax.ppermute(x, ("gy", "gx"), pairs)


def stage_kernel(mine_ref, out_ref):
    out_ref[...] = mine_ref[...]


def pair_kernel(mine_ref, theirs_ref, out_ref):
    out_ref[...] = jnp.concatenate([mine_ref[...], theirs_ref[...]], axis=0)


def stage(block):
    return pl.pallas_call(
        stage_kernel,
        out_shape=jax.ShapeDtypeStruct(block.shape, block.dtype),
        in_specs=in_vmem(1),
        out_specs=in_vmem(1)[0],
        compiler_params=pltpu.CompilerParams(vmem_limit_bytes=2 * MIB),
        cost_estimate=pl.CostEstimate(flops=1 << 35, bytes_accessed=1 << 17, transcendentals=0),
        name="stage",
    )(block)


def gather_rows(block, chips):
    half = chips // 2
    far = hop(block, chips, half)
    pair = pl.pallas_call(
        pair_kernel,
        out_shape=jax.ShapeDtypeStruct((2 * block.shape[0], block.shape[1]), block.dtype),
        in_specs=in_vmem(2),
        out_specs=in_vmem(1)[0],
        compiler_params=pltpu.CompilerParams(vmem_limit_bytes=2 * MIB),
        name="pair",
    )(hold(swap(block)), hold(far))
    return [block, swap(far)] + [hop(pair, chips, mask) for mask in range(1, half)]


def gather_early(block, staged, chips):
    half = chips // 2
    far = hop(block, chips, half)
    other = swap(block)
    masks = range(half - 1, 0, -1)
    near = {mask: hop(other, chips, mask) for mask in masks}
    beyond = {mask: hop(far, chips, mask) for mask in masks}
    pieces = [staged, swap(far)]
    for mask in range(1, half):
        pieces += [near[mask], beyond[mask]]
    return pieces


def project_kernel(*refs, swapped):
    *x_refs, w_ref, out_ref = refs
    heads = out_ref.shape[0]
    x = jnp.concatenate([x_ref[...] for x_ref in x_refs], axis=0)
    core = lax.axis_index("gx")
    first = heads * ((1 - core) if swapped else core)
    for head in range(heads):
        value = lax.dot_general(w_ref[first + head], x, NT, preferred_element_type=jnp.float32)
        out_ref[head] = value.T.astype(jnp.bfloat16)


def merge_kernel(near_ref, far_ref, back_ref, *out_refs):
    back_ref[...] = far_ref[0]
    for at, out_ref in enumerate(out_refs):
        mask = len(out_refs) - at
        out_ref[0] = near_ref[mask]
        out_ref[1] = far_ref[mask]


def attend_kernel(lengths_ref, near_ref, back_ref, *refs):
    *got_refs, key_ref, value_ref, out_ref, got, wide, tall, flat = refs
    half = len(got_refs) + 1
    seqs, heads, slots = key_ref.shape[0], key_ref.shape[1], key_ref.shape[2]
    part = got.shape[4]
    chip = lax.axis_index("gy")
    got[0, 0] = near_ref[0]
    got[0, 1] = back_ref[...]
    for at, got_ref in enumerate(got_refs):
        got[half - 1 - at] = got_ref[...]
    for other in range(2 * half):
        mask = chip ^ other
        piece = got[mask & (half - 1), mask // half]
        wide[:, :, other * part : (other + 1) * part] = piece.astype(jnp.float32)
    for column in range(GROUP + 2):
        for head in range(heads):
            tall[:, head, column, :] = wide[head, :, column * HD : (column + 1) * HD]
    scale = HD ** (-0.5)
    pairs = [(seq, head) for seq in range(seqs) for head in range(heads)]
    position = lax.broadcasted_iota(jnp.int32, (GROUP, slots), 1)
    queries, own, scores, live = [], [], [], []
    for seq, head in pairs:
        query = tall[seq, head, :GROUP, :]
        new_key = tall[seq, head, GROUP : GROUP + 1, :]
        own.append(jnp.sum(query * new_key, axis=1, keepdims=True))
        scores.append(
            lax.dot_general(
                query.astype(jnp.bfloat16), key_ref[seq, head], NT, preferred_element_type=jnp.float32
            )
        )
        live.append(jnp.where(position < lengths_ref[seq], 1.0, 0.0))
    live = jnp.concatenate(live, axis=0) > 0.5
    own = jnp.concatenate(own, axis=0) * scale
    scores = jnp.where(live, jnp.concatenate(scores, axis=0) * scale, NEG_FILL)
    top = jnp.maximum(jnp.max(scores, axis=1, keepdims=True), own)
    weights = jnp.where(live, jnp.exp(scores - top), 0.0)
    own_weight = jnp.exp(own - top)
    share = 1.0 / (jnp.sum(weights, axis=1, keepdims=True) + own_weight)
    weights = (weights * share).astype(jnp.bfloat16)
    own_weight = (own_weight * share).astype(jnp.bfloat16).astype(jnp.float32)
    for at, (seq, head) in enumerate(pairs):
        rows = slice(at * GROUP, (at + 1) * GROUP)
        mixed = jnp.dot(weights[rows], value_ref[seq, head], preferred_element_type=jnp.float32)
        mixed = mixed + own_weight[rows] * tall[seq, head, GROUP + 1 : GROUP + 2, :]
        for query_head in range(GROUP):
            column = (head * GROUP + query_head) * HD
            flat[seq : seq + 1, column : column + HD] = mixed[query_head : query_head + 1]
    out_ref[...] = flat[...].astype(jnp.bfloat16)


def output_kernel(*refs, rows):
    *x_refs, w_ref, keep_ref, send_ref = refs
    x = jnp.concatenate([x_ref[...] for x_ref in x_refs], axis=0)
    total = x.shape[0]
    half = total // (2 * rows)
    chip, core = lax.axis_index("gy"), lax.axis_index("gx")
    row = lax.broadcasted_iota(jnp.int32, (total, total), 0)
    column = lax.broadcasted_iota(jnp.int32, (total, total), 1)
    side, within = row // (half * rows), row % (half * rows)
    mask = chip ^ ((core ^ side) * half + within // rows)
    source = (mask % half) * (2 * rows) + (mask // half) * rows + within % rows
    order = jnp.where(column == source, 1.0, 0.0).astype(jnp.bfloat16)
    x = jnp.dot(order, x, preferred_element_type=jnp.float32).astype(jnp.bfloat16)
    cols = w_ref.shape[0]
    width = min(cols, 256)
    for at in range(0, cols, width):
        value = lax.dot_general(w_ref[at : at + width], x, NT, preferred_element_type=jnp.float32)
        value = value.T.astype(jnp.bfloat16)
        keep_ref[:, at : at + width] = value[: half * rows]
        send_ref[:, at : at + width] = value[half * rows :]


def in_vmem(count):
    return [pl.BlockSpec(memory_space=pltpu.VMEM)] * count


def hold(x):
    return pltpu.with_memory_space_constraint(x, pltpu.VMEM)


def local(activations, qkv_weight, out_weight, key_cache, value_cache, lengths, *, chips):
    _, part, width = qkv_weight.shape
    seqs, kv_local, slots, _ = key_cache.shape
    out_cols, feats = out_weight.shape
    half = chips // 2
    rows = chips * seqs
    limits = pltpu.CompilerParams(vmem_limit_bytes=8 * MIB)
    qkv_weight, out_weight = hold(qkv_weight), hold(out_weight)
    key_cache, value_cache = hold(key_cache), hold(value_cache)

    pieces = [hold(piece) for piece in gather_early(activations, stage(activations), chips)]

    def project(swapped):
        return pl.pallas_call(
            functools.partial(project_kernel, swapped=swapped),
            out_shape=jax.ShapeDtypeStruct((kv_local, rows, part), jnp.bfloat16),
            in_specs=in_vmem(chips + 1),
            out_specs=in_vmem(1)[0],
            compiler_params=limits,
            cost_estimate=pl.CostEstimate(
                flops=2 * kv_local * 256 * part * width, bytes_accessed=1 << 20, transcendentals=0
            ),
            name="project",
        )(*pieces, qkv_weight)

    arrived = swap(project(True))
    joined = (project(False).astype(jnp.float32) + arrived.astype(jnp.float32)).astype(jnp.bfloat16)
    joined = joined.reshape(kv_local, half, 2, seqs, part)
    near = jnp.stack([joined[:, mask, 0] for mask in range(half)])
    far = hop(jnp.stack([joined[:, mask, 1] for mask in range(half)]), chips, half)
    piece = jax.ShapeDtypeStruct((kv_local, seqs, part), jnp.bfloat16)
    pair = jax.ShapeDtypeStruct((2, kv_local, seqs, part), jnp.bfloat16)
    back, *pairs = pl.pallas_call(
        merge_kernel,
        out_shape=(piece,) + (pair,) * (half - 1),
        in_specs=in_vmem(2),
        out_specs=tuple(in_vmem(half)),
        compiler_params=pltpu.CompilerParams(vmem_limit_bytes=2 * MIB),
        name="merge",
    )(hold(swap(near)), hold(far))
    got = [hop(pair, chips, half - 1 - at) for at, pair in enumerate(pairs)]
    got = [near, swap(back)] + got

    attended = pl.pallas_call(
        attend_kernel,
        out_shape=jax.ShapeDtypeStruct((seqs, feats), jnp.bfloat16),
        in_specs=[pl.BlockSpec(memory_space=pltpu.SMEM)] + in_vmem(half + 3),
        out_specs=in_vmem(1)[0],
        scratch_shapes=[
            pltpu.VMEM((half, 2, kv_local, seqs, part), jnp.bfloat16),
            pltpu.VMEM((kv_local, seqs, chips * part), jnp.float32),
            pltpu.VMEM((seqs, kv_local, GROUP + 8, HD), jnp.float32),
            pltpu.VMEM((seqs, feats), jnp.float32),
        ],
        compiler_params=limits,
        name="attend",
    )(lengths, *[hold(piece) for piece in got], key_cache, value_cache)

    pieces = [hold(piece) for piece in gather_rows(attended, chips)]
    piece = jax.ShapeDtypeStruct((rows // 2, out_cols), jnp.bfloat16)
    keep, send = pl.pallas_call(
        functools.partial(output_kernel, rows=seqs),
        out_shape=(piece, piece),
        in_specs=in_vmem(half + 2),
        out_specs=tuple(in_vmem(2)),
        compiler_params=limits,
        name="output",
    )(*pieces, out_weight)
    return (keep.astype(jnp.float32) + swap(send).astype(jnp.float32)).astype(jnp.bfloat16)


def solution(mesh):
    in_specs = (
        P(("parts", "gy"), "gx"),
        P(None, "gy", "gx"),
        P("gy", "gx"),
        P(("parts", "gy"), "gx", None, None),
        P(("parts", "gy"), "gx", None, None),
        P(("parts", "gy")),
    )
    out_specs = P(("parts", "gx"), "gy")
    chips = mesh.shape["gy"]

    def whole(activations, qkv_weight, *rest):
        part = qkv_weight.shape[1] // chips
        seqs = activations.shape[0] // (mesh.shape["parts"] * chips)
        paired = mesh.shape["gx"] == 2 and chips in (2, 4, 8, 16) and part % 16 == 0
        paired = paired and seqs & (seqs - 1) == 0 and (chips // 2 * seqs) % 16 == 0
        body = functools.partial(local, chips=chips) if paired else local_plain
        return jax.shard_map(
            body, mesh=mesh, in_specs=in_specs, out_specs=out_specs, check_vma=False
        )(activations, qkv_weight, *rest)

    return whole
```

```python
import functools

import jax
import jax.numpy as jnp
from jax import lax
from jax.experimental import pallas as pl
from jax.experimental.pallas import tpu as pltpu
from jax.sharding import PartitionSpec as P

HD = 128
GROUP = 16
MIB = 1 << 20
NEG_FILL = -1e30
NT = (((1,), (1,)), ((), ()))


def normalize(scores, own_score, live):
    scores = jnp.where(live, scores, NEG_FILL)
    top = jnp.maximum(jnp.max(scores, axis=3), own_score)
    weights = jnp.where(live, jnp.exp(scores - top[..., None]), 0.0)
    own_weight = jnp.exp(own_score - top)
    denom = jnp.sum(weights, axis=3) + own_weight
    return (
        (weights / denom[..., None]).astype(jnp.bfloat16),
        (own_weight / denom).astype(jnp.bfloat16),
    )


def local_plain(activations, qkv_weight, out_weight, key_cache, value_cache, lengths):
    head_count, col_part, half_width = qkv_weight.shape
    flat_weight = qkv_weight.reshape(head_count * col_part, half_width)
    row_piece = lax.all_gather(activations, "gy", axis=0, tiled=True)
    product = lax.dot_general(row_piece, flat_weight, NT, preferred_element_type=jnp.float32)
    partial_value = product.reshape(row_piece.shape[0], head_count, col_part)
    summed = lax.psum_scatter(
        partial_value.astype(jnp.bfloat16), "gx", scatter_dimension=1, tiled=True
    )
    joined = lax.all_to_all(summed, "gy", split_axis=0, concat_axis=2, tiled=True)
    seq_local, kv_local, cache_len = (key_cache.shape[0], key_cache.shape[1], key_cache.shape[2])
    queries = joined[:, :, : GROUP * HD].reshape(seq_local, kv_local, GROUP, HD)
    new_key = joined[:, :, GROUP * HD : (GROUP + 1) * HD]
    new_value = joined[:, :, (GROUP + 1) * HD :]
    score_scale = HD ** (-0.5)
    own_score = (
        jnp.einsum("skgh,skh->skg", queries, new_key, preferred_element_type=jnp.float32)
        * score_scale
    )
    positions = jnp.arange(cache_len, dtype=jnp.int32)
    live = positions[None, None, None, :] < lengths[:, None, None, None]
    scores = (
        jnp.einsum("skgh,skth->skgt", queries, key_cache, preferred_element_type=jnp.float32)
        * score_scale
    )
    weights, own_weight = normalize(scores, own_score, live)
    mixed = jnp.einsum("skgt,skth->skgh", weights, value_cache, preferred_element_type=jnp.float32)
    mixed = (
        mixed
        + own_weight.astype(jnp.float32)[..., None] * new_value.astype(jnp.float32)[:, :, None, :]
    )
    attended = mixed.astype(jnp.bfloat16).reshape(seq_local, kv_local * GROUP * HD)
    terms = lax.dot_general(
        lax.all_gather(attended, "gy", axis=0, tiled=True),
        out_weight,
        NT,
        preferred_element_type=jnp.float32,
    )
    return lax.psum_scatter(terms.astype(jnp.bfloat16), "gx", scatter_dimension=0, tiled=True)


def swap(x):
    return lax.ppermute(x, "gx", [(0, 1), (1, 0)])


def hop(x, chips, mask):
    pairs = [(2 * g + c, 2 * (g ^ mask) + 1 - c) for g in range(chips) for c in range(2)]
    return lax.ppermute(x, ("gy", "gx"), pairs)


def stage_kernel(mine_ref, out_ref):
    out_ref[...] = mine_ref[...]


def pair_kernel(mine_ref, theirs_ref, out_ref):
    out_ref[...] = jnp.concatenate([mine_ref[...], theirs_ref[...]], axis=0)


def stage(block):
    return pl.pallas_call(
        stage_kernel,
        out_shape=jax.ShapeDtypeStruct(block.shape, block.dtype),
        in_specs=in_vmem(1),
        out_specs=in_vmem(1)[0],
        compiler_params=pltpu.CompilerParams(vmem_limit_bytes=2 * MIB),
        cost_estimate=pl.CostEstimate(flops=1 << 35, bytes_accessed=1 << 17, transcendentals=0),
        name="stage",
    )(block)


def gather_rows(block, chips):
    half = chips // 2
    far = hop(block, chips, half)
    pair = pl.pallas_call(
        pair_kernel,
        out_shape=jax.ShapeDtypeStruct((2 * block.shape[0], block.shape[1]), block.dtype),
        in_specs=in_vmem(2),
        out_specs=in_vmem(1)[0],
        compiler_params=pltpu.CompilerParams(vmem_limit_bytes=2 * MIB),
        name="pair",
    )(hold(swap(block)), hold(far))
    return [block, swap(far)] + [hop(pair, chips, mask) for mask in range(1, half)]


def gather_early(block, staged, chips):
    half = chips // 2
    far = hop(block, chips, half)
    other = swap(block)
    masks = range(half - 1, 0, -1)
    near = {mask: hop(other, chips, mask) for mask in masks}
    beyond = {mask: hop(far, chips, mask) for mask in masks}
    pieces = [staged, swap(far)]
    for mask in range(1, half):
        pieces += [near[mask], beyond[mask]]
    return pieces


def project_kernel(*refs, swapped):
    *x_refs, w_ref, out_ref = refs
    heads = out_ref.shape[0]
    x = jnp.concatenate([x_ref[...] for x_ref in x_refs], axis=0)
    core = lax.axis_index("gx")
    first = heads * ((1 - core) if swapped else core)
    for head in range(heads):
        value = lax.dot_general(w_ref[first + head], x, NT, preferred_element_type=jnp.float32)
        out_ref[head] = value.T.astype(jnp.bfloat16)


def sum_kernel(keep_ref, arrived_ref, near_ref, far_ref):
    half, _, seqs, _ = near_ref.shape
    total = keep_ref[...].astype(jnp.float32) + arrived_ref[...].astype(jnp.float32)
    for mask in range(half):
        at = 2 * seqs * mask
        near_ref[mask] = total[:, at : at + seqs].astype(jnp.bfloat16)
        far_ref[mask] = total[:, at + seqs : at + 2 * seqs].astype(jnp.bfloat16)


def merge_kernel(near_ref, far_ref, back_ref, *out_refs):
    back_ref[...] = far_ref[0]
    for at, out_ref in enumerate(out_refs):
        mask = len(out_refs) - at
        out_ref[0] = near_ref[mask]
        out_ref[1] = far_ref[mask]


def attend_kernel(lengths_ref, near_ref, back_ref, *refs):
    *got_refs, key_ref, value_ref, out_ref, got, wide, tall, flat = refs
    half = len(got_refs) + 1
    seqs, heads, slots = key_ref.shape[0], key_ref.shape[1], key_ref.shape[2]
    part = got.shape[4]
    chip = lax.axis_index("gy")
    got[0, 0] = near_ref[0]
    got[0, 1] = back_ref[...]
    for at, got_ref in enumerate(got_refs):
        got[half - 1 - at] = got_ref[...]
    for other in range(2 * half):
        mask = chip ^ other
        piece = got[mask & (half - 1), mask // half]
        wide[:, :, other * part : (other + 1) * part] = piece.astype(jnp.float32)
    for column in range(GROUP + 2):
        for head in range(heads):
            tall[:, head, column, :] = wide[head, :, column * HD : (column + 1) * HD]
    scale = HD ** (-0.5)
    pairs = [(seq, head) for seq in range(seqs) for head in range(heads)]
    position = lax.broadcasted_iota(jnp.int32, (GROUP, slots), 1)
    queries, own, scores, live = [], [], [], []
    for seq, head in pairs:
        query = tall[seq, head, :GROUP, :]
        new_key = tall[seq, head, GROUP : GROUP + 1, :]
        own.append(jnp.sum(query * new_key, axis=1, keepdims=True))
        scores.append(
            lax.dot_general(
                query.astype(jnp.bfloat16), key_ref[seq, head], NT, preferred_element_type=jnp.float32
            )
        )
        live.append(jnp.where(position < lengths_ref[seq], 1.0, 0.0))
    live = jnp.concatenate(live, axis=0) > 0.5
    own = jnp.concatenate(own, axis=0) * scale
    scores = jnp.where(live, jnp.concatenate(scores, axis=0) * scale, NEG_FILL)
    top = jnp.maximum(jnp.max(scores, axis=1, keepdims=True), own)
    weights = jnp.where(live, jnp.exp(scores - top), 0.0)
    own_weight = jnp.exp(own - top)
    share = 1.0 / (jnp.sum(weights, axis=1, keepdims=True) + own_weight)
    weights = (weights * share).astype(jnp.bfloat16)
    own_weight = (own_weight * share).astype(jnp.bfloat16).astype(jnp.float32)
    for at, (seq, head) in enumerate(pairs):
        rows = slice(at * GROUP, (at + 1) * GROUP)
        mixed = jnp.dot(weights[rows], value_ref[seq, head], preferred_element_type=jnp.float32)
        mixed = mixed + own_weight[rows] * tall[seq, head, GROUP + 1 : GROUP + 2, :]
        for query_head in range(GROUP):
            column = (head * GROUP + query_head) * HD
            flat[seq : seq + 1, column : column + HD] = mixed[query_head : query_head + 1]
    out_ref[...] = flat[...].astype(jnp.bfloat16)


def output_kernel(*refs, rows):
    *x_refs, w_ref, keep_ref, send_ref = refs
    x = jnp.concatenate([x_ref[...] for x_ref in x_refs], axis=0)
    total = x.shape[0]
    half = total // (2 * rows)
    chip, core = lax.axis_index("gy"), lax.axis_index("gx")
    row = lax.broadcasted_iota(jnp.int32, (total, total), 0)
    column = lax.broadcasted_iota(jnp.int32, (total, total), 1)
    side, within = row // (half * rows), row % (half * rows)
    mask = chip ^ ((core ^ side) * half + within // rows)
    source = (mask % half) * (2 * rows) + (mask // half) * rows + within % rows
    order = jnp.where(column == source, 1.0, 0.0).astype(jnp.bfloat16)
    x = jnp.dot(order, x, preferred_element_type=jnp.float32).astype(jnp.bfloat16)
    cols = w_ref.shape[0]
    width = min(cols, 256)
    for at in range(0, cols, width):
        value = lax.dot_general(w_ref[at : at + width], x, NT, preferred_element_type=jnp.float32)
        value = value.T.astype(jnp.bfloat16)
        keep_ref[:, at : at + width] = value[: half * rows]
        send_ref[:, at : at + width] = value[half * rows :]


def in_vmem(count):
    return [pl.BlockSpec(memory_space=pltpu.VMEM)] * count


def hold(x):
    return pltpu.with_memory_space_constraint(x, pltpu.VMEM)


def local(activations, qkv_weight, out_weight, key_cache, value_cache, lengths, *, chips):
    _, part, width = qkv_weight.shape
    seqs, kv_local, slots, _ = key_cache.shape
    out_cols, feats = out_weight.shape
    half = chips // 2
    rows = chips * seqs
    limits = pltpu.CompilerParams(vmem_limit_bytes=8 * MIB)
    qkv_weight, out_weight = hold(qkv_weight), hold(out_weight)
    key_cache, value_cache = hold(key_cache), hold(value_cache)

    pieces = [hold(piece) for piece in gather_early(activations, stage(activations), chips)]

    def project(swapped):
        return pl.pallas_call(
            functools.partial(project_kernel, swapped=swapped),
            out_shape=jax.ShapeDtypeStruct((kv_local, rows, part), jnp.bfloat16),
            in_specs=in_vmem(chips + 1),
            out_specs=in_vmem(1)[0],
            compiler_params=limits,
            cost_estimate=pl.CostEstimate(
                flops=2 * kv_local * 256 * part * width, bytes_accessed=1 << 20, transcendentals=0
            ),
            name="project",
        )(*pieces, qkv_weight)

    arrived = swap(project(True))
    stack = jax.ShapeDtypeStruct((half, kv_local, seqs, part), jnp.bfloat16)
    near, far = pl.pallas_call(
        sum_kernel,
        out_shape=(stack, stack),
        in_specs=in_vmem(2),
        out_specs=tuple(in_vmem(2)),
        compiler_params=pltpu.CompilerParams(vmem_limit_bytes=2 * MIB),
        name="sum",
    )(hold(project(False)), hold(arrived))
    far = hop(far, chips, half)
    piece = jax.ShapeDtypeStruct((kv_local, seqs, part), jnp.bfloat16)
    pair = jax.ShapeDtypeStruct((2, kv_local, seqs, part), jnp.bfloat16)
    back, *pairs = pl.pallas_call(
        merge_kernel,
        out_shape=(piece,) + (pair,) * (half - 1),
        in_specs=in_vmem(2),
        out_specs=tuple(in_vmem(half)),
        compiler_params=pltpu.CompilerParams(vmem_limit_bytes=2 * MIB),
        name="merge",
    )(hold(swap(near)), hold(far))
    got = [hop(pair, chips, half - 1 - at) for at, pair in enumerate(pairs)]
    got = [near, swap(back)] + got

    attended = pl.pallas_call(
        attend_kernel,
        out_shape=jax.ShapeDtypeStruct((seqs, feats), jnp.bfloat16),
        in_specs=[pl.BlockSpec(memory_space=pltpu.SMEM)] + in_vmem(half + 3),
        out_specs=in_vmem(1)[0],
        scratch_shapes=[
            pltpu.VMEM((half, 2, kv_local, seqs, part), jnp.bfloat16),
            pltpu.VMEM((kv_local, seqs, chips * part), jnp.float32),
            pltpu.VMEM((seqs, kv_local, GROUP + 8, HD), jnp.float32),
            pltpu.VMEM((seqs, feats), jnp.float32),
        ],
        compiler_params=limits,
        name="attend",
    )(lengths, *[hold(piece) for piece in got], key_cache, value_cache)

    pieces = [hold(piece) for piece in gather_rows(attended, chips)]
    piece = jax.ShapeDtypeStruct((rows // 2, out_cols), jnp.bfloat16)
    keep, send = pl.pallas_call(
        functools.partial(output_kernel, rows=seqs),
        out_shape=(piece, piece),
        in_specs=in_vmem(half + 2),
        out_specs=tuple(in_vmem(2)),
        compiler_params=limits,
        name="output",
    )(*pieces, out_weight)
    return (keep.astype(jnp.float32) + swap(send).astype(jnp.float32)).astype(jnp.bfloat16)


def solution(mesh):
    in_specs = (
        P(("parts", "gy"), "gx"),
        P(None, "gy", "gx"),
        P("gy", "gx"),
        P(("parts", "gy"), "gx", None, None),
        P(("parts", "gy"), "gx", None, None),
        P(("parts", "gy")),
    )
    out_specs = P(("parts", "gx"), "gy")
    chips = mesh.shape["gy"]

    def whole(activations, qkv_weight, *rest):
        part = qkv_weight.shape[1] // chips
        seqs = activations.shape[0] // (mesh.shape["parts"] * chips)
        paired = mesh.shape["gx"] == 2 and chips in (2, 4, 8, 16) and part % 16 == 0
        paired = paired and seqs & (seqs - 1) == 0 and (chips // 2 * seqs) % 16 == 0
        body = functools.partial(local, chips=chips) if paired else local_plain
        return jax.shard_map(
            body, mesh=mesh, in_specs=in_specs, out_specs=out_specs, check_vma=False
        )(activations, qkv_weight, *rest)

    return whole
```

```python
import functools

import jax
import jax.numpy as jnp
from jax import lax
from jax.experimental import pallas as pl
from jax.experimental.pallas import tpu as pltpu
from jax.sharding import PartitionSpec as P

HD = 128
GROUP = 16
MIB = 1 << 20
NEG_FILL = -1e30
NT = (((1,), (1,)), ((), ()))


def normalize(scores, own_score, live):
    scores = jnp.where(live, scores, NEG_FILL)
    top = jnp.maximum(jnp.max(scores, axis=3), own_score)
    weights = jnp.where(live, jnp.exp(scores - top[..., None]), 0.0)
    own_weight = jnp.exp(own_score - top)
    denom = jnp.sum(weights, axis=3) + own_weight
    return (
        (weights / denom[..., None]).astype(jnp.bfloat16),
        (own_weight / denom).astype(jnp.bfloat16),
    )


def local_plain(activations, qkv_weight, out_weight, key_cache, value_cache, lengths):
    head_count, col_part, half_width = qkv_weight.shape
    flat_weight = qkv_weight.reshape(head_count * col_part, half_width)
    row_piece = lax.all_gather(activations, "gy", axis=0, tiled=True)
    product = lax.dot_general(row_piece, flat_weight, NT, preferred_element_type=jnp.float32)
    partial_value = product.reshape(row_piece.shape[0], head_count, col_part)
    summed = lax.psum_scatter(
        partial_value.astype(jnp.bfloat16), "gx", scatter_dimension=1, tiled=True
    )
    joined = lax.all_to_all(summed, "gy", split_axis=0, concat_axis=2, tiled=True)
    seq_local, kv_local, cache_len = (key_cache.shape[0], key_cache.shape[1], key_cache.shape[2])
    queries = joined[:, :, : GROUP * HD].reshape(seq_local, kv_local, GROUP, HD)
    new_key = joined[:, :, GROUP * HD : (GROUP + 1) * HD]
    new_value = joined[:, :, (GROUP + 1) * HD :]
    score_scale = HD ** (-0.5)
    own_score = (
        jnp.einsum("skgh,skh->skg", queries, new_key, preferred_element_type=jnp.float32)
        * score_scale
    )
    positions = jnp.arange(cache_len, dtype=jnp.int32)
    live = positions[None, None, None, :] < lengths[:, None, None, None]
    scores = (
        jnp.einsum("skgh,skth->skgt", queries, key_cache, preferred_element_type=jnp.float32)
        * score_scale
    )
    weights, own_weight = normalize(scores, own_score, live)
    mixed = jnp.einsum("skgt,skth->skgh", weights, value_cache, preferred_element_type=jnp.float32)
    mixed = (
        mixed
        + own_weight.astype(jnp.float32)[..., None] * new_value.astype(jnp.float32)[:, :, None, :]
    )
    attended = mixed.astype(jnp.bfloat16).reshape(seq_local, kv_local * GROUP * HD)
    terms = lax.dot_general(
        lax.all_gather(attended, "gy", axis=0, tiled=True),
        out_weight,
        NT,
        preferred_element_type=jnp.float32,
    )
    return lax.psum_scatter(terms.astype(jnp.bfloat16), "gx", scatter_dimension=0, tiled=True)


def swap(x):
    return lax.ppermute(x, "gx", [(0, 1), (1, 0)])


def hop(x, chips, mask):
    pairs = [(2 * g + c, 2 * (g ^ mask) + 1 - c) for g in range(chips) for c in range(2)]
    return lax.ppermute(x, ("gy", "gx"), pairs)


def stage_kernel(mine_ref, out_ref):
    out_ref[...] = mine_ref[...]


def pair_kernel(mine_ref, theirs_ref, out_ref):
    out_ref[...] = jnp.concatenate([mine_ref[...], theirs_ref[...]], axis=0)


def stage(block):
    return pl.pallas_call(
        stage_kernel,
        out_shape=jax.ShapeDtypeStruct(block.shape, block.dtype),
        in_specs=in_vmem(1),
        out_specs=in_vmem(1)[0],
        compiler_params=pltpu.CompilerParams(vmem_limit_bytes=2 * MIB),
        cost_estimate=pl.CostEstimate(flops=1 << 35, bytes_accessed=1 << 17, transcendentals=0),
        name="stage",
    )(block)


def gather_rows(block, chips):
    half = chips // 2
    far = hop(block, chips, half)
    pair = pl.pallas_call(
        pair_kernel,
        out_shape=jax.ShapeDtypeStruct((2 * block.shape[0], block.shape[1]), block.dtype),
        in_specs=in_vmem(2),
        out_specs=in_vmem(1)[0],
        compiler_params=pltpu.CompilerParams(vmem_limit_bytes=2 * MIB),
        name="pair",
    )(hold(swap(block)), hold(far))
    return [block, swap(far)] + [hop(pair, chips, mask) for mask in range(1, half)]


def gather_early(block, staged, chips):
    half = chips // 2
    far = hop(block, chips, half)
    other = swap(block)
    masks = range(half - 1, 0, -1)
    near = {mask: hop(other, chips, mask) for mask in masks}
    beyond = {mask: hop(far, chips, mask) for mask in masks}
    pieces = [staged, swap(far)]
    for mask in range(1, half):
        pieces += [near[mask], beyond[mask]]
    return pieces


def project_kernel(*refs, swapped):
    *x_refs, w_ref, out_ref = refs
    heads = out_ref.shape[0]
    x = jnp.concatenate([x_ref[...] for x_ref in x_refs], axis=0)
    core = lax.axis_index("gx")
    first = heads * ((1 - core) if swapped else core)
    for head in range(heads):
        value = lax.dot_general(w_ref[first + head], x, NT, preferred_element_type=jnp.float32)
        out_ref[head] = value.T.astype(jnp.bfloat16)


def sum_kernel(keep_ref, arrived_ref, near_ref, far_ref):
    half, _, seqs, _ = near_ref.shape
    total = keep_ref[...].astype(jnp.float32) + arrived_ref[...].astype(jnp.float32)
    for mask in range(half):
        at = 2 * seqs * mask
        near_ref[mask] = total[:, at : at + seqs].astype(jnp.bfloat16)
        far_ref[mask] = total[:, at + seqs : at + 2 * seqs].astype(jnp.bfloat16)


def merge_kernel(near_ref, far_ref, back_ref, *out_refs):
    back_ref[...] = far_ref[0]
    for at, out_ref in enumerate(out_refs):
        mask = len(out_refs) - at
        out_ref[0] = near_ref[mask]
        out_ref[1] = far_ref[mask]


def attend_kernel(lengths_ref, near_ref, back_ref, *refs):
    *got_refs, key_ref, value_ref, out_ref, got, wide, tall, flat = refs
    half = len(got_refs) + 1
    seqs, heads, slots = key_ref.shape[0], key_ref.shape[1], key_ref.shape[2]
    part = got.shape[4]
    chip = lax.axis_index("gy")
    got[0, 0] = near_ref[0]
    got[0, 1] = back_ref[...]
    for at, got_ref in enumerate(got_refs):
        got[half - 1 - at] = got_ref[...]
    for other in range(2 * half):
        mask = chip ^ other
        piece = got[mask & (half - 1), mask // half]
        wide[:, :, other * part : (other + 1) * part] = piece.astype(jnp.float32)
    for column in range(GROUP + 2):
        for head in range(heads):
            tall[:, head, column, :] = wide[head, :, column * HD : (column + 1) * HD]
    scale = HD ** (-0.5)
    pairs = [(seq, head) for seq in range(seqs) for head in range(heads)]
    position = lax.broadcasted_iota(jnp.int32, (GROUP, slots), 1)
    queries, own, scores, live = [], [], [], []
    for seq, head in pairs:
        query = tall[seq, head, :GROUP, :]
        new_key = tall[seq, head, GROUP : GROUP + 1, :]
        own.append(jnp.sum(query * new_key, axis=1, keepdims=True))
        scores.append(
            lax.dot_general(
                query.astype(jnp.bfloat16), key_ref[seq, head], NT, preferred_element_type=jnp.float32
            )
        )
        live.append(jnp.where(position < lengths_ref[seq], 1.0, 0.0))
    live = jnp.concatenate(live, axis=0) > 0.5
    own = jnp.concatenate(own, axis=0) * scale
    scores = jnp.where(live, jnp.concatenate(scores, axis=0) * scale, NEG_FILL)
    top = jnp.maximum(jnp.max(scores, axis=1, keepdims=True), own)
    weights = jnp.where(live, jnp.exp(scores - top), 0.0)
    own_weight = jnp.exp(own - top)
    share = 1.0 / (jnp.sum(weights, axis=1, keepdims=True) + own_weight)
    weights = (weights * share).astype(jnp.bfloat16)
    own_weight = (own_weight * share).astype(jnp.bfloat16).astype(jnp.float32)
    for at, (seq, head) in enumerate(pairs):
        rows = slice(at * GROUP, (at + 1) * GROUP)
        mixed = jnp.dot(weights[rows], value_ref[seq, head], preferred_element_type=jnp.float32)
        mixed = mixed + own_weight[rows] * tall[seq, head, GROUP + 1 : GROUP + 2, :]
        for query_head in range(GROUP):
            column = (head * GROUP + query_head) * HD
            flat[seq : seq + 1, column : column + HD] = mixed[query_head : query_head + 1]
    out_ref[...] = flat[...].astype(jnp.bfloat16)


def output_kernel(*refs):
    own_ref, back_ref, *pair_refs, w_ref, keep_ref, send_ref, placed = refs
    chips, rows = placed.shape[0], placed.shape[1]
    half = chips // 2
    chip, core = lax.axis_index("gy"), lax.axis_index("gx")

    def place(mask, block):
        source = chip ^ mask
        side = core ^ (source // half)
        placed[side * half + source % half] = block.astype(jnp.float32)

    place(0, own_ref[...])
    place(half, back_ref[...])
    for at, pair_ref in enumerate(pair_refs):
        pair = pair_ref[...].astype(jnp.float32)
        place(at + 1, pair[:rows])
        place(at + 1 + half, pair[rows:])
    x = jnp.concatenate([placed[at] for at in range(chips)], axis=0).astype(jnp.bfloat16)
    cols = w_ref.shape[0]
    width = min(cols, 256)
    for at in range(0, cols, width):
        value = lax.dot_general(w_ref[at : at + width], x, NT, preferred_element_type=jnp.float32)
        value = value.T.astype(jnp.bfloat16)
        keep_ref[:, at : at + width] = value[: half * rows]
        send_ref[:, at : at + width] = value[half * rows :]


def in_vmem(count):
    return [pl.BlockSpec(memory_space=pltpu.VMEM)] * count


def hold(x):
    return pltpu.with_memory_space_constraint(x, pltpu.VMEM)


def local(activations, qkv_weight, out_weight, key_cache, value_cache, lengths, *, chips):
    _, part, width = qkv_weight.shape
    seqs, kv_local, slots, _ = key_cache.shape
    out_cols, feats = out_weight.shape
    half = chips // 2
    rows = chips * seqs
    limits = pltpu.CompilerParams(vmem_limit_bytes=8 * MIB)
    qkv_weight, out_weight = hold(qkv_weight), hold(out_weight)
    key_cache, value_cache = hold(key_cache), hold(value_cache)

    pieces = [hold(piece) for piece in gather_early(activations, stage(activations), chips)]

    def project(swapped):
        return pl.pallas_call(
            functools.partial(project_kernel, swapped=swapped),
            out_shape=jax.ShapeDtypeStruct((kv_local, rows, part), jnp.bfloat16),
            in_specs=in_vmem(chips + 1),
            out_specs=in_vmem(1)[0],
            compiler_params=limits,
            cost_estimate=pl.CostEstimate(
                flops=2 * kv_local * 256 * part * width, bytes_accessed=1 << 20, transcendentals=0
            ),
            name="project",
        )(*pieces, qkv_weight)

    arrived = swap(project(True))
    stack = jax.ShapeDtypeStruct((half, kv_local, seqs, part), jnp.bfloat16)
    near, far = pl.pallas_call(
        sum_kernel,
        out_shape=(stack, stack),
        in_specs=in_vmem(2),
        out_specs=tuple(in_vmem(2)),
        compiler_params=pltpu.CompilerParams(vmem_limit_bytes=2 * MIB),
        name="sum",
    )(hold(project(False)), hold(arrived))
    far = hop(far, chips, half)
    piece = jax.ShapeDtypeStruct((kv_local, seqs, part), jnp.bfloat16)
    pair = jax.ShapeDtypeStruct((2, kv_local, seqs, part), jnp.bfloat16)
    back, *pairs = pl.pallas_call(
        merge_kernel,
        out_shape=(piece,) + (pair,) * (half - 1),
        in_specs=in_vmem(2),
        out_specs=tuple(in_vmem(half)),
        compiler_params=pltpu.CompilerParams(vmem_limit_bytes=2 * MIB),
        name="merge",
    )(hold(swap(near)), hold(far))
    got = [hop(pair, chips, half - 1 - at) for at, pair in enumerate(pairs)]
    got = [near, swap(back)] + got

    attended = pl.pallas_call(
        attend_kernel,
        out_shape=jax.ShapeDtypeStruct((seqs, feats), jnp.bfloat16),
        in_specs=[pl.BlockSpec(memory_space=pltpu.SMEM)] + in_vmem(half + 3),
        out_specs=in_vmem(1)[0],
        scratch_shapes=[
            pltpu.VMEM((half, 2, kv_local, seqs, part), jnp.bfloat16),
            pltpu.VMEM((kv_local, seqs, chips * part), jnp.float32),
            pltpu.VMEM((seqs, kv_local, GROUP + 8, HD), jnp.float32),
            pltpu.VMEM((seqs, feats), jnp.float32),
        ],
        compiler_params=limits,
        name="attend",
    )(lengths, *[hold(piece) for piece in got], key_cache, value_cache)

    pieces = [hold(piece) for piece in gather_rows(attended, chips)]
    piece = jax.ShapeDtypeStruct((rows // 2, out_cols), jnp.bfloat16)
    keep, send = pl.pallas_call(
        output_kernel,
        out_shape=(piece, piece),
        in_specs=in_vmem(half + 2),
        out_specs=tuple(in_vmem(2)),
        scratch_shapes=[pltpu.VMEM((chips, seqs, feats), jnp.float32)],
        compiler_params=limits,
        name="output",
    )(*pieces, out_weight)
    return (keep.astype(jnp.float32) + swap(send).astype(jnp.float32)).astype(jnp.bfloat16)


def solution(mesh):
    in_specs = (
        P(("parts", "gy"), "gx"),
        P(None, "gy", "gx"),
        P("gy", "gx"),
        P(("parts", "gy"), "gx", None, None),
        P(("parts", "gy"), "gx", None, None),
        P(("parts", "gy")),
    )
    out_specs = P(("parts", "gx"), "gy")
    chips = mesh.shape["gy"]

    def whole(activations, qkv_weight, *rest):
        part = qkv_weight.shape[1] // chips
        seqs = activations.shape[0] // (mesh.shape["parts"] * chips)
        paired = mesh.shape["gx"] == 2 and chips in (2, 4, 8, 16) and part % 16 == 0
        paired = paired and seqs & (seqs - 1) == 0 and (chips // 2 * seqs) % 16 == 0
        body = functools.partial(local, chips=chips) if paired else local_plain
        return jax.shard_map(
            body, mesh=mesh, in_specs=in_specs, out_specs=out_specs, check_vma=False
        )(activations, qkv_weight, *rest)

    return whole
```
